256 devices in a mesh: dp: 32 (over y, x, core), seq: 8 (over z).
Axes of the slice: x: 4, y: 4, z: 8, core: 2. Of those that a mesh axis runs over, the one named last changes fastest.
Arguments:
- query: bfloat16 [32768, 8192], P(('dp', 'seq')), may hold values from -40 to 40, as said below
- key_projection: bfloat16 [32768, 1024], P(('dp', 'seq')), may hold values from -40 to 40, as said below
- value: bfloat16 [32768, 1024], P(('dp', 'seq')), may hold values from -6 to 6
- d_out: bfloat16 [32768, 8192], P(('dp', 'seq')), may hold values from -6 to 6
- q_gain: float32 [128], replicated, may hold values from 0.1 to 1.9
- key_norm_gain: float32 [128], replicated, may hold values from 0.1 to 1.9
- seq_lengths: int32 [32, 3], P('dp'), may hold values from 1 to 512, 1024 in all within a row
- send_order: int32 [32, 8, 128], P('dp', 'seq'), may hold values from 0 to 127, each once within a row
- recv_order: int32 [32, 8, 128], P('dp', 'seq'), may hold values from 0 to 127, each once within a row
Outputs:
- attn_out: bfloat16 [32768, 8192], P(('dp', 'seq'))
- d_query: bfloat16 [32768, 8192], P(('dp', 'seq'))
- d_key: bfloat16 [32768, 1024], P(('dp', 'seq'))
- d_value: bfloat16 [32768, 1024], P(('dp', 'seq'))
The draws below stay inside these ranges and needn't reach their ends.
Inputs may be any that keep to these rules, and one draw needn't show every extreme that they name: query is bounded in magnitude. key_projection is bounded in magnitude. `seq_lengths`: each group's 3 lengths sum to 1024, and the largest of each group is 512. `send_order`: each device's 128 entries are a permutation. `recv_order`: each device's 128 entries are a permutation.
All inputs are finite; a program needn't handle non-finite values.
Results may differ from the reference program's by a relative error of at most 0.0083.
Values may be sent and summed in bfloat16 or wider, within the bound.
No kernel may reach another device: no remote copies, remote signals or barrier semaphores. Data moves between devices by JAX's collectives and lax.ppermute only.
A program may use at most 128 MiB of HBM per device.

```python
import math
import jax
import jax.numpy as jnp
import numpy as np
from jax import lax

QUERY_HEADS = 64
KEY_VALUE_HEADS = 8
HEAD_SIZE = 128
TOK_DEV = 128
SEQS_G = 3
GROUPS = 32
GROUP_DEVS = 8
GROUP_TOK = 1024
MAXLEN = 512
TOKEN_COUNT = 32768


def draw_query(key, part):
    key = jax.random.fold_in(key, 11)
    first_result, second_result, third_result = jax.random.split(key, 3)
    start_offset = jnp.clip(jax.random.normal(first_result, (TOKEN_COUNT, QUERY_HEADS, HEAD_SIZE), jnp.float32), -4.0, 4.0)
    row_list = jnp.exp(jax.random.uniform(second_result, (TOKEN_COUNT, QUERY_HEADS, 1), jnp.float32, 0.0, math.log(3.16)))
    column_list = jnp.exp(jax.random.uniform(third_result, (1, QUERY_HEADS, HEAD_SIZE), jnp.float32, 0.0, math.log(3.16)))
    return (start_offset * row_list * column_list).reshape(TOKEN_COUNT, QUERY_HEADS * HEAD_SIZE).astype(jnp.bfloat16)


def draw_key_projection(key, part):
    key = jax.random.fold_in(key, 23)
    first_result, second_result, third_result = jax.random.split(key, 3)
    start_offset = jnp.clip(jax.random.normal(first_result, (TOKEN_COUNT, KEY_VALUE_HEADS, HEAD_SIZE), jnp.float32), -4.0, 4.0)
    row_list = jnp.exp(jax.random.uniform(second_result, (TOKEN_COUNT, KEY_VALUE_HEADS, 1), jnp.float32, 0.0, math.log(3.16)))
    column_list = jnp.exp(jax.random.uniform(third_result, (1, KEY_VALUE_HEADS, HEAD_SIZE), jnp.float32, 0.0, math.log(3.16)))
    return (start_offset * row_list * column_list).reshape(TOKEN_COUNT, KEY_VALUE_HEADS * HEAD_SIZE).astype(jnp.bfloat16)


def block_levels(stream_key, extent, cuts, least, top_value):
    def one(dim, blocks):
        heights = jax.random.uniform(jax.random.fold_in(jax.random.fold_in(stream_key, 6), dim), (blocks,), jnp.float32, least / len(cuts), top_value / len(cuts))
        return jnp.repeat(jnp.exp(heights), extent[dim] // blocks).reshape((-1,) + (1,) * (len(extent) - dim - 1))

    factor_of = one(*cuts[0])
    for cut in cuts[1:]:
        factor_of = factor_of * one(*cut)
    return factor_of


def profile(count, total, bound, skew):
    loads = [(1 << 20) // math.isqrt(standing ** skew) + 1 for standing in range(2, count + 1)]
    spare, holding = total - bound - (count - 1), [1] * (count - 1)
    while spare > 0:
        movable = [i for i in range(count - 1) if holding[i] < bound]
        mass, left = sum([loads[i] for i in movable]), spare
        for i in movable:
            extra = min(bound - holding[i], max(1, left * loads[i] // mass), spare)
            holding[i] = holding[i] + extra
            spare = spare - extra
    return np.array([bound] + holding)


def ragged_sizes(stream_key, count, total, most, lean):
    if count == 2:
        one = jax.random.randint(stream_key, (), max(1, total - most), min(most, total - 1) + 1)
        return jnp.stack([one, total - one])
    sizes = jnp.asarray(profile(count, total, most, lean), jnp.int32)
    twos = (count - 1) // 2
    source_of, receiver = sizes[1:1 + 2 * twos:2], sizes[2:2 + 2 * twos:2]
    margin = jnp.minimum(source_of - 1, most - receiver)
    moved = jax.random.randint(jax.random.fold_in(stream_key, 1), (twos,), 0, 1 << 20) % (margin + 1)
    sizes = sizes.at[1:1 + 2 * twos:2].set(source_of - moved).at[2:2 + 2 * twos:2].set(receiver + moved)
    return sizes[jax.random.permutation(jax.random.fold_in(stream_key, 2), count)]


def normal_values(rng, dims, scale, most, pieces=(), kind=jnp.bfloat16):
    values = scale * jax.random.normal(rng, dims, jnp.float32)
    if pieces:
        values = values * block_levels(rng, dims, pieces, -0.22, 0.18)
    return jnp.clip(values, -most, most).astype(kind)


def setup_inputs(seed: int = 0) -> dict:
    streams_of = jax.random.split(jax.random.key(seed), 10)
    return {
        "query": draw_query(jax.random.fold_in(streams_of[9], 71), 0),
        "key_projection": draw_key_projection(jax.random.fold_in(streams_of[9], 71), 0),
        "value": normal_values(streams_of[2], (TOKEN_COUNT, KEY_VALUE_HEADS * HEAD_SIZE), 1.0, 6.0, ((0, 256),)),
        "d_out": normal_values(streams_of[3], (TOKEN_COUNT, QUERY_HEADS * HEAD_SIZE), 1.0, 6.0, ((0, 256),)),
        "q_gain": jnp.clip(1.0 + 0.18 * jax.random.normal(streams_of[4], (HEAD_SIZE,), jnp.float32), 0.1, 1.9),
        "key_norm_gain": jnp.clip(1.0 + 0.18 * jax.random.normal(streams_of[5], (HEAD_SIZE,), jnp.float32), 0.1, 1.9),
        "seq_lengths": jax.vmap(lambda own: ragged_sizes(own, SEQS_G, GROUP_TOK, MAXLEN, 2))(jax.random.split(streams_of[6], GROUPS)).reshape((GROUPS, SEQS_G)).astype(jnp.int32),
        "send_order": jax.vmap(lambda own: jax.random.permutation(own, TOK_DEV))(jax.random.split(streams_of[7], GROUPS * GROUP_DEVS)).reshape((GROUPS, GROUP_DEVS, TOK_DEV)).astype(jnp.int32),
        "recv_order": jax.vmap(lambda own: jax.random.permutation(own, TOK_DEV))(jax.random.split(streams_of[8], GROUPS * GROUP_DEVS)).reshape((GROUPS, GROUP_DEVS, TOK_DEV)).astype(jnp.int32),
    }


EPS = 1e-06

def apply_norm(row_list, gain, heads):
    shaped = row_list.reshape(row_list.shape[0], heads, -1)
    factor = lax.rsqrt(lax.optimization_barrier(jnp.mean(shaped * shaped, axis=-1, keepdims=True)) + EPS)
    return (shaped * factor * gain).reshape(row_list.shape[0], -1)

def to_packed(row_list, send_order, recv_order):
    width = row_list.shape[-1]
    share = TOK_DEV // GROUPS
    shaped = row_list.reshape(GROUPS, GROUP_DEVS, TOK_DEV, width)
    sent = jnp.take_along_axis(shaped, send_order[..., None], axis=2)
    received = sent.reshape(GROUPS, GROUP_DEVS, GROUPS, share, width).transpose(2, 1, 0, 3, 4)
    received = received.reshape(GROUPS, GROUP_DEVS, TOK_DEV, width)
    packed = jnp.take_along_axis(received, recv_order[..., None], axis=2)
    return packed.reshape(GROUPS, GROUP_TOK, width)

def from_packed(packed, send_order, recv_order):
    width = packed.shape[-1]
    share = TOK_DEV // GROUPS
    shaped = packed.reshape(GROUPS, GROUP_DEVS, TOK_DEV, width)
    undo_recv = jnp.argsort(recv_order, axis=-1).astype(jnp.int32)
    received = jnp.take_along_axis(shaped, undo_recv[..., None], axis=2)
    sent = received.reshape(GROUPS, GROUP_DEVS, GROUPS, share, width).transpose(2, 1, 0, 3, 4)
    sent = sent.reshape(GROUPS, GROUP_DEVS, TOK_DEV, width)
    undo_send = jnp.argsort(send_order, axis=-1).astype(jnp.int32)
    row_list = jnp.take_along_axis(sent, undo_send[..., None], axis=2)
    return row_list.reshape(TOKEN_COUNT, width)

def group_attention(parts):
    query_row_list, key_row_list, value_row_list, rows_gradient, lengths = parts
    grand_total = query_row_list.shape[0]
    query_group_ratio = QUERY_HEADS // KEY_VALUE_HEADS
    scale = HEAD_SIZE ** (-0.5)
    ends = jnp.cumsum(lengths).astype(jnp.int32)
    position = jnp.arange(grand_total, dtype=jnp.int32)
    segment = lax.optimization_barrier(jnp.sum((position[:, None] >= ends[None, :]).astype(jnp.int32), axis=1))
    visible = (segment[:, None] == segment[None, :]) & (position[None, :] <= position[:, None])
    query_head_split = query_row_list.reshape(grand_total, KEY_VALUE_HEADS, query_group_ratio, HEAD_SIZE).transpose(1, 2, 0, 3)
    heads_gradient = rows_gradient.reshape(grand_total, KEY_VALUE_HEADS, query_group_ratio, HEAD_SIZE).transpose(1, 2, 0, 3)
    key_head_split = key_row_list.reshape(grand_total, KEY_VALUE_HEADS, HEAD_SIZE).transpose(1, 0, 2)
    value_head_split = value_row_list.reshape(grand_total, KEY_VALUE_HEADS, HEAD_SIZE).transpose(1, 0, 2)

    def one_head(items):
        qh, kh, vh, dh = items
        qf = qh.astype(jnp.float32)
        kf = kh.astype(jnp.float32)
        vf = vh.astype(jnp.float32)
        df = dh.astype(jnp.float32)
        scores = jnp.einsum('hqd,kd->hqk', qf, kf) * scale
        expo = jnp.where(visible[None], jnp.exp(scores), 0.0)
        weights = expo / lax.optimization_barrier(jnp.sum(expo, axis=-1, keepdims=True))
        weights_low = lax.optimization_barrier(weights.astype(jnp.bfloat16))
        out = lax.optimization_barrier(jnp.einsum('hqk,kd->hqd', weights_low.astype(jnp.float32), vf).astype(jnp.bfloat16))
        delta = lax.optimization_barrier(jnp.sum(df * out.astype(jnp.float32), axis=-1, keepdims=True))
        d_weights = jnp.einsum('hqd,kd->hqk', df, vf)
        d_scores = lax.optimization_barrier((weights * (d_weights - delta)).astype(jnp.bfloat16))
        dsf = d_scores.astype(jnp.float32)
        d_q = (jnp.einsum('hqk,kd->hqd', dsf, kf) * scale).astype(jnp.bfloat16)
        key_gradient = (jnp.einsum('hqk,hqd->kd', dsf, qf) * scale).astype(jnp.bfloat16)
        value_gradient = jnp.einsum('hqk,hqd->kd', weights_low.astype(jnp.float32), df).astype(jnp.bfloat16)
        return (out, d_q, key_gradient, value_gradient)
    out, d_q, key_gradient, value_gradient = lax.map(one_head, (query_head_split, key_head_split, value_head_split, heads_gradient))
    out = out.transpose(2, 0, 1, 3).reshape(grand_total, QUERY_HEADS * HEAD_SIZE)
    d_q = d_q.transpose(2, 0, 1, 3).reshape(grand_total, QUERY_HEADS * HEAD_SIZE)
    key_gradient = key_gradient.transpose(1, 0, 2).reshape(grand_total, KEY_VALUE_HEADS * HEAD_SIZE)
    value_gradient = value_gradient.transpose(1, 0, 2).reshape(grand_total, KEY_VALUE_HEADS * HEAD_SIZE)
    return (out, d_q, key_gradient, value_gradient)

def reference(query, key_projection, value, d_out, q_gain, key_norm_gain, seq_lengths, send_order, recv_order):
    q_float = query.astype(jnp.float32)
    key_single = key_projection.astype(jnp.float32)
    qn_float, q_pull = jax.vjp(lambda input_tensor: apply_norm(input_tensor, q_gain, QUERY_HEADS), q_float)
    key_normed_single, key_fetcher = jax.vjp(lambda input_tensor: apply_norm(input_tensor, key_norm_gain, KEY_VALUE_HEADS), key_single)
    qn = qn_float.astype(jnp.bfloat16)
    kn = key_normed_single.astype(jnp.bfloat16)
    q_packed = to_packed(qn, send_order, recv_order)
    k_packed = to_packed(kn, send_order, recv_order)
    v_packed = to_packed(value, send_order, recv_order)
    d_packed = to_packed(d_out, send_order, recv_order)
    out, d_q, key_gradient, value_gradient = lax.map(group_attention, (q_packed, k_packed, v_packed, d_packed, seq_lengths))
    attn_out = from_packed(out, send_order, recv_order)
    dqn = lax.optimization_barrier(from_packed(d_q, send_order, recv_order))
    dkn = lax.optimization_barrier(from_packed(key_gradient, send_order, recv_order))
    d_value = from_packed(value_gradient, send_order, recv_order)
    d_query = q_pull(dqn.astype(jnp.float32))[0].astype(jnp.bfloat16)
    d_key = key_fetcher(dkn.astype(jnp.float32))[0].astype(jnp.bfloat16)
    return (attn_out, d_query, d_key, d_value)
```

```python
import functools

import jax
import jax.numpy as jnp
from jax import lax
from jax.experimental import pallas as pl
from jax.experimental.pallas import tpu as pltpu
from jax.sharding import PartitionSpec as P

Q_HEADS = 64
KV_HEADS = 8
HEAD = 128
RATIO = Q_HEADS // KV_HEADS
EPS = 1e-06
ROWS = 128
GROUPS = 32
SHARE = ROWS // GROUPS
SPLIT = 4
CHUNK = SHARE * SPLIT
TALL = GROUPS * CHUNK
WIDE = 2 * HEAD
BACK = 4
WINDOW = (BACK + 1) * ROWS
SCALE = HEAD ** (-0.5)
LOG2E = 1.4426950408889634
FIRST = 6
VMEM_LIMIT = 40 * 1024 * 1024
F32 = jnp.float32
BF16 = jnp.bfloat16


def params():
    return pltpu.CompilerParams(vmem_limit_bytes=VMEM_LIMIT)


def cost(flops, moved, trans=0):
    return pl.CostEstimate(flops=int(flops), bytes_accessed=int(moved), transcendentals=int(trans))


def dot(a, b, dims):
    return lax.dot_general(a, b, (dims, ((), ())), preferred_element_type=F32)


MM = ((1,), (0,))
MT = ((1,), (1,))
TM = ((0,), (0,))


def iota(shape, dim):
    return lax.broadcasted_iota(jnp.int32, shape, dim)


def tall_row(index):
    row = (index // CHUNK) * SHARE + index % SHARE
    part = (index // SHARE) % SPLIT
    return row, part


def home_matrix(order_ref):
    spread_row, _ = tall_row(iota((ROWS, TALL), 1))
    spread = (spread_row == iota((ROWS, TALL), 0)).astype(BF16)
    order = jnp.broadcast_to(order_ref[...].astype(F32), (16, ROWS)).astype(BF16)
    source = dot(order, spread, MM)[:1]
    _, part = tall_row(iota((1, TALL), 1))
    code = source + (part * ROWS).astype(F32)
    return (iota((TALL, TALL), 0).astype(F32) == code).astype(BF16)


def pack_matrix(order_ref):
    row, part = tall_row(iota((TALL, SPLIT * ROWS), 0))
    order = order_ref[...]
    code = jnp.concatenate([order + p * ROWS for p in range(SPLIT)], axis=1)
    return (row + part * ROWS == code).astype(BF16)


def norm(x, gain):
    factor = lax.rsqrt(jnp.mean(x * x, axis=-1, keepdims=True) + EPS)
    return x * factor * gain


def norm_back(x, gain, dy):
    factor = lax.rsqrt(jnp.mean(x * x, axis=-1, keepdims=True) + EPS)
    g = dy * gain
    inner = jnp.mean(x * g, axis=-1, keepdims=True)
    return factor * g - x * (factor * factor * factor * inner)


def head_cols(h):
    return slice(h * HEAD, (h + 1) * HEAD)


def send_kv_kernel(order_ref, gain_ref, k_ref, v_ref, out_ref):
    gain = gain_ref[...]
    kn = [
        norm(k_ref[:, head_cols(h)].astype(F32), gain).astype(BF16) for h in range(KV_HEADS)
    ]
    half = KV_HEADS * HEAD // 2
    stack = jnp.concatenate(
        [
            jnp.concatenate(kn[: KV_HEADS // 2], axis=1),
            jnp.concatenate(kn[KV_HEADS // 2 :], axis=1),
            v_ref[:, :half],
            v_ref[:, half:],
        ],
        axis=0,
    )
    sent = dot(home_matrix(order_ref), stack, TM).astype(BF16)
    out_ref[...] = sent.reshape(GROUPS, CHUNK, half)


def send_kv(order, gain, key_projection, value):
    half = KV_HEADS * HEAD // 2
    return pl.pallas_call(
        send_kv_kernel,
        out_shape=jax.ShapeDtypeStruct((GROUPS, CHUNK, half), BF16),
        compiler_params=params(),
        cost_estimate=cost(2 * TALL * TALL * half, 3 << 19),
        name="send_kv",
    )(order, gain, key_projection, value)


def send_rows_kernel(order_ref, gain_ref, q_ref, d_ref, out_ref, home_ref):
    @pl.when(pl.program_id(0) == 0)
    def _():
        home_ref[...] = home_matrix(order_ref)

    gain = gain_ref[...]
    qn = [norm(q_ref[:, head_cols(h)].astype(F32), gain).astype(BF16) for h in range(RATIO)]
    stack = jnp.concatenate(
        [
            jnp.concatenate(
                [qn[2 * p], qn[2 * p + 1], d_ref[:, p * WIDE : (p + 1) * WIDE]], axis=1
            )
            for p in range(SPLIT)
        ],
        axis=0,
    )
    sent = dot(home_ref[...], stack, TM).astype(BF16)
    out_ref[...] = sent.reshape(GROUPS, CHUNK, 2 * WIDE)


def send_rows(order, gain, query, d_out, first, count):
    return pl.pallas_call(
        send_rows_kernel,
        grid=(count,),
        in_specs=[
            pl.BlockSpec((1, ROWS), lambda h: (0, 0)),
            pl.BlockSpec((1, HEAD), lambda h: (0, 0)),
            pl.BlockSpec((ROWS, RATIO * HEAD), lambda h: (0, h + first)),
            pl.BlockSpec((ROWS, RATIO * HEAD), lambda h: (0, h + first)),
        ],
        out_specs=pl.BlockSpec((GROUPS, CHUNK, 2 * WIDE), lambda h: (0, 0, h)),
        out_shape=jax.ShapeDtypeStruct((GROUPS, CHUNK, count * 2 * WIDE), BF16),
        scratch_shapes=[pltpu.VMEM((TALL, TALL), BF16)],
        compiler_params=params(),
        cost_estimate=cost(count * 2 * TALL * TALL * 2 * WIDE, count << 20),
        name="send_rows",
    )(order, gain, query, d_out)


def sort_kv_kernel(order_ref, in_ref, first_ref, last_ref):
    half = KV_HEADS * HEAD // 2
    rows = dot(pack_matrix(order_ref), in_ref[...].reshape(TALL, half), TM).astype(BF16)
    for h in range(KV_HEADS):
        ref, at = (first_ref, h) if h < FIRST else (last_ref, h - FIRST)
        part, cols = h // (KV_HEADS // 2), head_cols(h % (KV_HEADS // 2))
        k = rows[part * ROWS : (part + 1) * ROWS, cols]
        v = rows[(part + 2) * ROWS : (part + 3) * ROWS, cols]
        ref[:, at * WIDE : (at + 1) * WIDE] = jnp.concatenate([k, v], axis=1)


def sort_kv(order, received):
    return pl.pallas_call(
        sort_kv_kernel,
        out_shape=[
            jax.ShapeDtypeStruct((ROWS, count * WIDE), BF16)
            for count in (FIRST, KV_HEADS - FIRST)
        ],
        compiler_params=params(),
        cost_estimate=cost(2 * TALL**3, 1 << 20),
        name="sort_kv",
    )(order, received)


def attend_kernel(meta_ref, order_ref, qd_ref, *refs):
    kv_refs = refs[: BACK + 1]
    out_ref = refs[BACK + 1]
    part_refs = refs[BACK + 2 : 2 * BACK + 3]
    bias_ref = refs[2 * BACK + 3]

    @pl.when(pl.program_id(0) == 0)
    def _():
        row, _ = tall_row(iota((TALL, ROWS), 0))
        hit = row == order_ref[...]
        position = jnp.sum(
            jnp.where(hit, iota((TALL, ROWS), 1).astype(F32), 0.0), axis=1, keepdims=True
        )
        base = meta_ref[3] * ROWS
        position = position + base.astype(F32)
        end0 = meta_ref[0].astype(F32)
        end1 = (meta_ref[0] + meta_ref[1]).astype(F32)
        start = jnp.where(position < end0, 0.0, jnp.where(position < end1, end0, end1))
        key = (iota((TALL, WINDOW), 1) + (base - BACK * ROWS)).astype(F32)
        bias_ref[...] = jnp.where((key >= start) & (key <= position), 0.0, -1e30)

    kw = jnp.concatenate([r[:, :HEAD] for r in kv_refs], axis=0)
    vw = jnp.concatenate([r[:, HEAD:] for r in kv_refs], axis=0)
    dk = jnp.zeros((WINDOW, HEAD), F32)
    dv = jnp.zeros((WINDOW, HEAD), F32)
    step = TALL // 2
    for e in range(2):
        for low in range(0, TALL, step):
            g0, g1 = low // CHUNK, (low + step) // CHUNK
            q = qd_ref[g0:g1, :, e * HEAD : (e + 1) * HEAD].reshape(step, HEAD)
            d = qd_ref[g0:g1, :, WIDE + e * HEAD : WIDE + (e + 1) * HEAD].reshape(step, HEAD)
            scores = dot(q, kw, MT)
            expo = jnp.exp2(scores * (SCALE * LOG2E) + bias_ref[low : low + step, :])
            weights = expo * (1.0 / jnp.sum(expo, axis=-1, keepdims=True))
            low_weights = weights.astype(BF16)
            out = dot(low_weights, vw, MM).astype(BF16)
            delta = jnp.sum(d.astype(F32) * out.astype(F32), axis=-1, keepdims=True)
            d_weights = dot(d, vw, MT)
            d_scores = (weights * (d_weights - delta)).astype(BF16)
            dq = (dot(d_scores, kw, MM) * SCALE).astype(BF16)
            dk = dk + dot(d_scores, q, TM)
            dv = dv + dot(low_weights, d, TM)
            out_ref[g0:g1, :, e * HEAD : (e + 1) * HEAD] = out.reshape(g1 - g0, CHUNK, HEAD)
            out_ref[g0:g1, :, WIDE + e * HEAD : WIDE + (e + 1) * HEAD] = dq.reshape(
                g1 - g0, CHUNK, HEAD
            )
    dk = dk * SCALE
    for n, ref in enumerate(part_refs):
        ref[:, :HEAD] = dk[n * ROWS : (n + 1) * ROWS].astype(ref.dtype)
        ref[:, HEAD:] = dv[n * ROWS : (n + 1) * ROWS].astype(ref.dtype)


def attend(meta, order, received, blocks, count):
    kv_spec = pl.BlockSpec((ROWS, WIDE), lambda h: (0, h))
    elements = count * RATIO * ROWS * WINDOW
    return pl.pallas_call(
        attend_kernel,
        grid=(count,),
        in_specs=[
            pl.BlockSpec(memory_space=pltpu.SMEM),
            pl.BlockSpec((1, ROWS), lambda h: (0, 0)),
            pl.BlockSpec((GROUPS, CHUNK, 2 * WIDE), lambda h: (0, 0, h)),
        ]
        + [kv_spec] * (BACK + 1),
        out_specs=[pl.BlockSpec((GROUPS, CHUNK, 2 * WIDE), lambda h: (0, 0, h))]
        + [kv_spec] * (BACK + 1),
        out_shape=[jax.ShapeDtypeStruct((GROUPS, CHUNK, count * 2 * WIDE), BF16)]
        + [
            jax.ShapeDtypeStruct((ROWS, count * WIDE), BF16 if n == 0 else F32)
            for n in range(BACK + 1)
        ],
        scratch_shapes=[pltpu.VMEM((TALL, WINDOW), F32)],
        compiler_params=params(),
        cost_estimate=cost(12 * elements * HEAD, count * (3 << 20), elements),
        name="attend",
    )(meta, order, received, *blocks)


def return_kv_kernel(order_ref, *refs):
    first, last, sums, out_ref = refs[0], refs[1], refs[2:4], refs[4]
    total = [
        jnp.concatenate(
            [
                (r[...].astype(F32) + p[...]).astype(BF16)
                for r, p in zip((first, last), sums)
            ],
            axis=1,
        )
    ][0]
    quarter = KV_HEADS // 2
    rows = []
    for which in range(2):
        for part in range(2):
            rows.append(
                jnp.concatenate(
                    [
                        total[:, h * WIDE + which * HEAD : h * WIDE + (which + 1) * HEAD]
                        for h in range(part * quarter, (part + 1) * quarter)
                    ],
                    axis=1,
                )
            )
    stack = jnp.concatenate(rows, axis=0)
    out_ref[...] = (
        dot(pack_matrix(order_ref), stack, MM)
        .astype(BF16)
        .reshape(GROUPS, CHUNK, quarter * HEAD)
    )


def return_kv(order, first, last, own_first, own_last):
    half = KV_HEADS * HEAD // 2
    return pl.pallas_call(
        return_kv_kernel,
        out_shape=jax.ShapeDtypeStruct((GROUPS, CHUNK, half), BF16),
        compiler_params=params(),
        cost_estimate=cost(2 * TALL**3, 3 << 20),
        name="return_kv",
    )(order, first, last, own_first, own_last)


def finish_rows_kernel(order_ref, gain_ref, q_ref, in_ref, *refs):
    out_ref, dq_ref, home_ref = refs[-3:]

    @pl.when(pl.program_id(0) == 0)
    def _():
        home_ref[...] = home_matrix(order_ref)

    gain = gain_ref[...]
    rows = dot(home_ref[...], in_ref[...].reshape(TALL, 2 * WIDE), MM)
    for part in range(SPLIT):
        mine = rows[part * ROWS : (part + 1) * ROWS]
        cols = slice(part * WIDE, (part + 1) * WIDE)
        out_ref[:, cols] = mine[:, :WIDE].astype(BF16)
        for e in range(2):
            at = slice(part * WIDE + e * HEAD, part * WIDE + (e + 1) * HEAD)
            dy = mine[:, WIDE + e * HEAD : WIDE + (e + 1) * HEAD]
            dq_ref[:, at] = norm_back(q_ref[:, at].astype(F32), gain, dy).astype(BF16)


def finish_rows(order, gain, query, received, first, count, earlier=()):
    block = pl.BlockSpec((ROWS, RATIO * HEAD), lambda h: (0, h + first))
    whole = jax.ShapeDtypeStruct((ROWS, Q_HEADS * HEAD), BF16)
    return pl.pallas_call(
        finish_rows_kernel,
        grid=(count,),
        in_specs=[
            pl.BlockSpec((1, ROWS), lambda h: (0, 0)),
            pl.BlockSpec((1, HEAD), lambda h: (0, 0)),
            block,
            pl.BlockSpec((GROUPS, CHUNK, 2 * WIDE), lambda h: (0, 0, h)),
        ]
        + [pl.BlockSpec(memory_space=pl.ANY)] * len(earlier),
        out_specs=[block, block],
        out_shape=[whole, whole],
        scratch_shapes=[pltpu.VMEM((TALL, TALL), BF16)],
        input_output_aliases={4 + n: n for n in range(len(earlier))},
        compiler_params=params(),
        cost_estimate=cost(count * 2 * TALL * TALL * 2 * WIDE, count * (5 << 18)),
        name="finish_rows",
    )(order, gain, query, received, *earlier)


def finish_kv_kernel(order_ref, gain_ref, k_ref, in_ref, dk_ref, dv_ref):
    half = KV_HEADS * HEAD // 2
    gain = gain_ref[...]
    rows = dot(home_matrix(order_ref), in_ref[...].reshape(TALL, half), MM)
    for h in range(KV_HEADS):
        part, cols = h // (KV_HEADS // 2), head_cols(h % (KV_HEADS // 2))
        dy = rows[part * ROWS : (part + 1) * ROWS, cols]
        dk_ref[:, head_cols(h)] = norm_back(
            k_ref[:, head_cols(h)].astype(F32), gain, dy
        ).astype(BF16)
    dv_ref[:, :half] = rows[2 * ROWS : 3 * ROWS].astype(BF16)
    dv_ref[:, half:] = rows[3 * ROWS :].astype(BF16)


def finish_kv(order, gain, key_projection, received):
    half = KV_HEADS * HEAD // 2
    columns = received.shape[2] // half
    block = pl.BlockSpec((ROWS, KV_HEADS * HEAD), lambda i: (0, 0))
    whole = jax.ShapeDtypeStruct((ROWS, KV_HEADS * HEAD), BF16)
    return pl.pallas_call(
        finish_kv_kernel,
        grid=(1,),
        in_specs=[
            pl.BlockSpec((1, ROWS), lambda i: (0, 0)),
            pl.BlockSpec((1, HEAD), lambda i: (0, 0)),
            block,
            pl.BlockSpec((GROUPS, CHUNK, half), lambda i: (0, 0, columns - 1)),
        ],
        out_specs=[block, block],
        out_shape=[whole, whole],
        compiler_params=params(),
        cost_estimate=cost(2 * TALL**3, 3 << 19),
        name="finish_kv",
    )(order, gain, key_projection, received)


def exchange(array):
    return lax.all_to_all(array, "dp", split_axis=0, concat_axis=0, tiled=True)


def along(array, step):
    count = lax.axis_size("seq")
    return lax.ppermute(array, "seq", [(i, (i + step) % count) for i in range(count)])


def per_device(
    query, key_projection, value, d_out, q_gain, key_norm_gain, seq_lengths, send_order, recv_order
):
    leaving = send_order.reshape(1, ROWS)
    arriving = recv_order.reshape(1, ROWS)
    q_gain = q_gain.reshape(1, HEAD)
    k_gain = key_norm_gain.reshape(1, HEAD)
    place = lax.axis_index("seq").astype(jnp.int32)
    meta = jnp.concatenate([seq_lengths[0], place[None]])
    counts = (FIRST, KV_HEADS - FIRST)
    starts = (0, FIRST)

    kv_sent = send_kv(leaving, k_gain, key_projection, value)
    kv_received = exchange(kv_sent)
    sent = [
        send_rows(leaving, q_gain, query, d_out, first, count)
        for first, count in zip(starts, counts)
    ]
    kv_received, sent[0] = lax.optimization_barrier((kv_received, sent[0]))
    received_first = exchange(sent[0])
    received_first, sent[1] = lax.optimization_barrier((received_first, sent[1]))
    received = [received_first, exchange(sent[1])]

    chains = []
    for block in sort_kv(arriving, kv_received):
        chain = [block]
        for _ in range(BACK):
            chain.append(along(chain[-1], 1))
        chains.append(chain[::-1])

    results, totals, own = [], [], []
    for n in range(2):
        result, *parts = attend(meta, arriving, received[n], chains[n], counts[n])
        total = parts[0]
        for part in parts[1:-1]:
            total = (along(total, -1).astype(F32) + part).astype(BF16)
        totals.append(along(total, -1))
        own.append(parts[-1])
        results.append(result)

    back_first = exchange(results[0])
    kv_back = return_kv(arriving, totals[0], totals[1], own[0], own[1])
    kv_back, results[1], back_first = lax.optimization_barrier((kv_back, results[1], back_first))
    back_last = exchange(jnp.concatenate([results[1], kv_back], axis=2))

    outs = finish_rows(leaving, q_gain, query, back_first, starts[0], counts[0])
    attn_out, d_query = finish_rows(
        leaving, q_gain, query, back_last, starts[1], counts[1], earlier=outs
    )
    d_key, d_value = finish_kv(leaving, k_gain, key_projection, back_last)
    return attn_out, d_query, d_key, d_value


def solution(mesh):
    rows = P(("dp", "seq"), None)
    in_specs = (rows, rows, rows, rows, P(), P(), P("dp", None)) + (P("dp", "seq", None),) * 2
    return jax.shard_map(
        per_device, mesh=mesh, in_specs=in_specs, out_specs=(rows,) * 4, check_vma=False
    )
```

```python
import functools

import jax
import jax.numpy as jnp
from jax import lax
from jax.experimental import pallas as pl
from jax.experimental.pallas import tpu as pltpu
from jax.sharding import PartitionSpec as P

Q_HEADS = 64
KV_HEADS = 8
HEAD = 128
RATIO = Q_HEADS // KV_HEADS
EPS = 1e-06
ROWS = 128
GROUPS = 32
SHARE = ROWS // GROUPS
SPLIT = 4
CHUNK = SHARE * SPLIT
TALL = GROUPS * CHUNK
WIDE = 2 * HEAD
BACK = 4
WINDOW = (BACK + 1) * ROWS
SCALE = HEAD ** (-0.5)
LOG2E = 1.4426950408889634
FIRST = 6
VMEM_LIMIT = 52 * 1024 * 1024
VMEM_WHOLE = 62 * 1024 * 1024
F32 = jnp.float32
BF16 = jnp.bfloat16


def params(limit=VMEM_LIMIT):
    return pltpu.CompilerParams(vmem_limit_bytes=limit)


def cost(flops, moved, trans=0):
    return pl.CostEstimate(flops=int(flops), bytes_accessed=int(moved), transcendentals=int(trans))


def dot(a, b, dims):
    return lax.dot_general(a, b, (dims, ((), ())), preferred_element_type=F32)


MM = ((1,), (0,))
MT = ((1,), (1,))
TM = ((0,), (0,))


def iota(shape, dim):
    return lax.broadcasted_iota(jnp.int32, shape, dim)


def tall_row(index):
    row = (index // CHUNK) * SHARE + index % SHARE
    part = (index // SHARE) % SPLIT
    return row, part


def home_matrix(order_ref):
    spread_row, _ = tall_row(iota((ROWS, TALL), 1))
    spread = (spread_row == iota((ROWS, TALL), 0)).astype(BF16)
    order = jnp.broadcast_to(order_ref[...].astype(F32), (16, ROWS)).astype(BF16)
    source = dot(order, spread, MM)[:1]
    _, part = tall_row(iota((1, TALL), 1))
    code = source + (part * ROWS).astype(F32)
    return (iota((TALL, TALL), 0).astype(F32) == code).astype(BF16)


def pack_matrix(order_ref):
    row, part = tall_row(iota((TALL, SPLIT * ROWS), 0))
    order = order_ref[...]
    code = jnp.concatenate([order + p * ROWS for p in range(SPLIT)], axis=1)
    return (row + part * ROWS == code).astype(BF16)


def norm(x, gain):
    factor = lax.rsqrt(jnp.mean(x * x, axis=-1, keepdims=True) + EPS)
    return x * factor * gain


def norm_back(x, gain, dy):
    factor = lax.rsqrt(jnp.mean(x * x, axis=-1, keepdims=True) + EPS)
    g = dy * gain
    inner = jnp.mean(x * g, axis=-1, keepdims=True)
    return factor * g - x * (factor * factor * factor * inner)


def head_cols(h):
    return slice(h * HEAD, (h + 1) * HEAD)


def send_kv_kernel(order_ref, gain_ref, k_ref, v_ref, out_ref):
    gain = gain_ref[...]
    kn = [
        norm(k_ref[:, head_cols(h)].astype(F32), gain).astype(BF16) for h in range(KV_HEADS)
    ]
    half = KV_HEADS * HEAD // 2
    stack = jnp.concatenate(
        [
            jnp.concatenate(kn[: KV_HEADS // 2], axis=1),
            jnp.concatenate(kn[KV_HEADS // 2 :], axis=1),
            v_ref[:, :half],
            v_ref[:, half:],
        ],
        axis=0,
    )
    sent = dot(home_matrix(order_ref), stack, TM).astype(BF16)
    out_ref[...] = sent.reshape(GROUPS, CHUNK, half)


def send_kv(order, gain, key_projection, value):
    half = KV_HEADS * HEAD // 2
    return pl.pallas_call(
        send_kv_kernel,
        out_shape=jax.ShapeDtypeStruct((GROUPS, CHUNK, half), BF16),
        compiler_params=params(VMEM_WHOLE),
        cost_estimate=cost(2 * TALL * TALL * half, 3 << 19),
        name="send_kv",
    )(order, gain, key_projection, value)


def send_rows_kernel(order_ref, gain_ref, q_ref, d_ref, out_ref, home_ref):
    @pl.when(pl.program_id(0) == 0)
    def _():
        home_ref[...] = home_matrix(order_ref)

    gain = gain_ref[...]
    qn = [norm(q_ref[:, head_cols(h)].astype(F32), gain).astype(BF16) for h in range(RATIO)]
    stack = jnp.concatenate(
        [
            jnp.concatenate(
                [qn[2 * p], qn[2 * p + 1], d_ref[:, p * WIDE : (p + 1) * WIDE]], axis=1
            )
            for p in range(SPLIT)
        ],
        axis=0,
    )
    sent = dot(home_ref[...], stack, TM).astype(BF16)
    out_ref[...] = sent.reshape(GROUPS, CHUNK, 2 * WIDE)


def send_rows(order, gain, query, d_out, first, count):
    return pl.pallas_call(
        send_rows_kernel,
        grid=(count,),
        in_specs=[
            pl.BlockSpec((1, ROWS), lambda h: (0, 0)),
            pl.BlockSpec((1, HEAD), lambda h: (0, 0)),
            pl.BlockSpec((ROWS, RATIO * HEAD), lambda h: (0, h + first)),
            pl.BlockSpec((ROWS, RATIO * HEAD), lambda h: (0, h + first)),
        ],
        out_specs=pl.BlockSpec((GROUPS, CHUNK, 2 * WIDE), lambda h: (0, 0, h)),
        out_shape=jax.ShapeDtypeStruct((GROUPS, CHUNK, count * 2 * WIDE), BF16),
        scratch_shapes=[pltpu.VMEM((TALL, TALL), BF16)],
        compiler_params=params(VMEM_WHOLE),
        cost_estimate=cost(count * 2 * TALL * TALL * 2 * WIDE, count << 20),
        name="send_rows",
    )(order, gain, query, d_out)


def sort_kv_kernel(order_ref, in_ref, first_ref, last_ref):
    half = KV_HEADS * HEAD // 2
    rows = dot(pack_matrix(order_ref), in_ref[...].reshape(TALL, half), TM).astype(BF16)
    for h in range(KV_HEADS):
        ref, at = (first_ref, h) if h < FIRST else (last_ref, h - FIRST)
        part, cols = h // (KV_HEADS // 2), head_cols(h % (KV_HEADS // 2))
        k = rows[part * ROWS : (part + 1) * ROWS, cols]
        v = rows[(part + 2) * ROWS : (part + 3) * ROWS, cols]
        ref[:, at * WIDE : (at + 1) * WIDE] = jnp.concatenate([k, v], axis=1)


def sort_kv(order, received):
    return pl.pallas_call(
        sort_kv_kernel,
        out_shape=[
            jax.ShapeDtypeStruct((ROWS, count * WIDE), BF16)
            for count in (FIRST, KV_HEADS - FIRST)
        ],
        compiler_params=params(),
        cost_estimate=cost(2 * TALL**3, 1 << 20),
        name="sort_kv",
    )(order, received)


def attend_kernel(meta_ref, order_ref, qd_ref, *refs):
    kv_refs = refs[: BACK + 1]
    out_ref = refs[BACK + 1]
    part_refs = refs[BACK + 2 : 2 * BACK + 3]
    bias_ref = refs[2 * BACK + 3]

    @pl.when(pl.program_id(0) == 0)
    def _():
        places = jnp.broadcast_to(iota((1, ROWS), 1).astype(F32), (16, ROWS)).astype(BF16)
        arrived = (iota((ROWS, ROWS), 0) == order_ref[...]).astype(BF16)
        place = dot(places, arrived, MT).astype(BF16)
        row, _ = tall_row(iota((ROWS, TALL), 1))
        spread = (row == iota((ROWS, TALL), 0)).astype(BF16)
        base = meta_ref[3] * ROWS
        position = dot(place, spread, MM)[:1] + base.astype(F32)
        end0 = meta_ref[0].astype(F32)
        end1 = (meta_ref[0] + meta_ref[1]).astype(F32)
        start = jnp.where(position < end0, 0.0, jnp.where(position < end1, end0, end1))
        key = (iota((WINDOW, TALL), 0) + (base - BACK * ROWS)).astype(F32)
        bias_ref[...] = jnp.where((key >= start) & (key <= position), 0.0, -1e30)

    kw = jnp.concatenate([r[:, :HEAD] for r in kv_refs], axis=0)
    vw = jnp.concatenate([r[:, HEAD:] for r in kv_refs], axis=0)

    def both(low):
        return jnp.concatenate(
            [
                qd_ref[:, :, low + e * HEAD : low + (e + 1) * HEAD].reshape(TALL, HEAD)
                for e in range(2)
            ],
            axis=0,
        )

    q, d = both(0), both(WIDE)
    scores = dot(kw, q, MT)
    d_weights = dot(vw, d, MT)
    bias = bias_ref[...]
    expo = jnp.exp2(scores * (SCALE * LOG2E) + jnp.concatenate([bias, bias], axis=1))
    weights = expo * (1.0 / jnp.sum(expo, axis=0, keepdims=True))
    low_weights = weights.astype(BF16)
    out = dot(vw, low_weights, TM).astype(BF16)
    delta = jnp.sum(d.astype(F32).T * out.astype(F32), axis=0, keepdims=True)
    d_scores = (weights * (d_weights - delta)).astype(BF16)
    dq = (dot(kw, d_scores, TM) * SCALE).astype(BF16)
    dk = dot(d_scores, q, MM) * SCALE
    dv = dot(low_weights, d, MM)
    for low, value in ((0, out.T), (WIDE, dq.T)):
        for e in range(2):
            out_ref[:, :, low + e * HEAD : low + (e + 1) * HEAD] = value[
                e * TALL : (e + 1) * TALL
            ].reshape(GROUPS, CHUNK, HEAD)
    for n, ref in enumerate(part_refs):
        ref[:, :HEAD] = dk[n * ROWS : (n + 1) * ROWS].astype(ref.dtype)
        ref[:, HEAD:] = dv[n * ROWS : (n + 1) * ROWS].astype(ref.dtype)


def attend(meta, order, received, blocks, count, room=0):
    kv_spec = pl.BlockSpec((ROWS, WIDE), lambda h: (0, h))
    elements = count * RATIO * ROWS * WINDOW
    return pl.pallas_call(
        attend_kernel,
        grid=(count,),
        in_specs=[
            pl.BlockSpec(memory_space=pltpu.SMEM),
            pl.BlockSpec((1, ROWS), lambda h: (0, 0)),
            pl.BlockSpec((GROUPS, CHUNK, 2 * WIDE), lambda h: (0, 0, h)),
        ]
        + [kv_spec] * (BACK + 1),
        out_specs=[pl.BlockSpec((GROUPS, CHUNK, 2 * WIDE), lambda h: (0, 0, h))]
        + [kv_spec] * (BACK + 1),
        out_shape=[jax.ShapeDtypeStruct((GROUPS, CHUNK, (count + room) * 2 * WIDE), BF16)]
        + [
            jax.ShapeDtypeStruct((ROWS, count * WIDE), BF16 if n == 0 else F32)
            for n in range(BACK + 1)
        ],
        scratch_shapes=[pltpu.VMEM((WINDOW, TALL), F32)],
        compiler_params=params(),
        cost_estimate=cost(12 * elements * HEAD, count * (3 << 20), elements),
        name="attend",
    )(meta, order, received, *blocks)


def return_kv_kernel(order_ref, first_ref, last_ref, own_first_ref, own_last_ref, _, out_ref):
    half = KV_HEADS * HEAD // 2
    total = jnp.concatenate(
        [
            (got[...].astype(F32) + own[...]).astype(BF16)
            for got, own in ((first_ref, own_first_ref), (last_ref, own_last_ref))
        ],
        axis=1,
    )

    def columns(which, part):
        heads = range(part * KV_HEADS // 2, (part + 1) * KV_HEADS // 2)
        return jnp.concatenate([total[:, head_cols(2 * h + which)] for h in heads], axis=1)

    stack = jnp.concatenate(
        [columns(which, part) for which in range(2) for part in range(2)], axis=0
    )
    rows = dot(pack_matrix(order_ref), stack, MM).astype(BF16)
    out_ref[...] = rows.reshape(GROUPS, CHUNK, half)


def return_kv(order, first, last, own_first, own_last, result):
    half = KV_HEADS * HEAD // 2
    place = result.shape[2] // half - 1
    small = [pl.BlockSpec(a.shape, lambda i: (0, 0)) for a in (first, last, own_first, own_last)]
    return pl.pallas_call(
        return_kv_kernel,
        grid=(1,),
        in_specs=[pl.BlockSpec((1, ROWS), lambda i: (0, 0)), *small]
        + [pl.BlockSpec(memory_space=pl.ANY)],
        out_specs=pl.BlockSpec((GROUPS, CHUNK, half), lambda i: (0, 0, place)),
        out_shape=jax.ShapeDtypeStruct(result.shape, BF16),
        input_output_aliases={5: 0},
        compiler_params=params(),
        cost_estimate=cost(2 * TALL**3, 3 << 20),
        name="return_kv",
    )(order, first, last, own_first, own_last, result)


def finish_rows_step(rows, gain, q_ref, out_ref, dq_ref):
    for part in range(SPLIT):
        mine = rows[part * ROWS : (part + 1) * ROWS]
        out_ref[:, part * WIDE : (part + 1) * WIDE] = mine[:, :WIDE].astype(BF16)
        for e in range(2):
            at = head_cols(2 * part + e)
            dy = mine[:, WIDE + e * HEAD : WIDE + (e + 1) * HEAD]
            dq_ref[:, at] = norm_back(q_ref[:, at].astype(F32), gain, dy).astype(BF16)


def finish_kv_step(rows, gain, k_ref, dk_ref, dv_ref):
    half = KV_HEADS * HEAD // 2
    for h in range(KV_HEADS):
        part, cols = h // (KV_HEADS // 2), head_cols(h % (KV_HEADS // 2))
        dy = rows[part * ROWS : (part + 1) * ROWS, cols]
        dk_ref[:, head_cols(h)] = norm_back(
            k_ref[:, head_cols(h)].astype(F32), gain, dy
        ).astype(BF16)
    dv_ref[:, :half] = rows[2 * ROWS : 3 * ROWS].astype(BF16)
    dv_ref[:, half:] = rows[3 * ROWS :].astype(BF16)


def finish_kernel(with_kv, order_ref, gain_ref, q_ref, in_ref, *refs):
    home_ref = refs[-1]
    step = pl.program_id(0)

    @pl.when(step == 0)
    def _():
        home_ref[...] = home_matrix(order_ref)

    rows = dot(home_ref[...], in_ref[...].reshape(TALL, 2 * WIDE), MM)
    if with_kv:
        k_gain_ref, k_ref, _, _, out_ref, dq_ref, dk_ref, dv_ref = refs[:-1]
        last = pl.num_programs(0) - 1

        @pl.when(step < last)
        def _():
            finish_rows_step(rows, gain_ref[...], q_ref, out_ref, dq_ref)

        @pl.when(step == last)
        def _():
            finish_kv_step(rows, k_gain_ref[...], k_ref, dk_ref, dv_ref)
    else:
        out_ref, dq_ref = refs[:-1]
        finish_rows_step(rows, gain_ref[...], q_ref, out_ref, dq_ref)


def finish(order, gain, query, received, first, count, kv=(), earlier=()):
    block = pl.BlockSpec((ROWS, RATIO * HEAD), lambda h: (0, jnp.minimum(h, count - 1) + first))
    whole = jax.ShapeDtypeStruct((ROWS, Q_HEADS * HEAD), BF16)
    row = pl.BlockSpec((1, ROWS), lambda h: (0, 0))
    kv_block = pl.BlockSpec((ROWS, KV_HEADS * HEAD), lambda h: (0, 0))
    kv_whole = jax.ShapeDtypeStruct((ROWS, KV_HEADS * HEAD), BF16)
    in_specs = [row, row, block, pl.BlockSpec((GROUPS, CHUNK, 2 * WIDE), lambda h: (0, 0, h))]
    if kv:
        in_specs += [row, kv_block] + [pl.BlockSpec(memory_space=pl.ANY)] * 2
    return pl.pallas_call(
        functools.partial(finish_kernel, bool(kv)),
        grid=(count + 1 if kv else count,),
        in_specs=in_specs,
        out_specs=[block, block] + ([kv_block] * 2 if kv else []),
        out_shape=[whole, whole] + ([kv_whole] * 2 if kv else []),
        scratch_shapes=[pltpu.VMEM((TALL, TALL), BF16)],
        input_output_aliases={6: 0, 7: 1} if kv else {},
        compiler_params=params(),
        cost_estimate=cost(count * 2 * TALL * TALL * 2 * WIDE, count * (5 << 18)),
        name="finish",
    )(order, gain, query, received, *kv, *earlier)


def exchange(array):
    return lax.all_to_all(array, "dp", split_axis=0, concat_axis=0, tiled=True)


def along(array, step):
    count = lax.axis_size("seq")
    return lax.ppermute(array, "seq", [(i, (i + step) % count) for i in range(count)])


def after(array, other):
    return lax.optimization_barrier((array, other))[0]


def per_device(
    query, key_projection, value, d_out, q_gain, key_norm_gain, seq_lengths, send_order, recv_order
):
    leaving = send_order.reshape(1, ROWS)
    arriving = recv_order.reshape(1, ROWS)
    q_gain = q_gain.reshape(1, HEAD)
    k_gain = key_norm_gain.reshape(1, HEAD)
    place = lax.axis_index("seq").astype(jnp.int32)
    meta = jnp.concatenate([seq_lengths[0], place[None]])
    counts = (FIRST, KV_HEADS - FIRST)
    starts = (0, FIRST)

    kv_sent = send_kv(leaving, k_gain, key_projection, value)
    kv_received = exchange(kv_sent)
    sent = [
        send_rows(leaving, q_gain, query, d_out, first, count)
        for first, count in zip(starts, counts)
    ]
    kv_received, *sent = lax.optimization_barrier((kv_received, *sent))
    received_first = exchange(sent[0])
    received_first, last = lax.optimization_barrier((received_first, sent[1]))
    received = [received_first, exchange(last)]

    firsts, lasts = ([block] for block in sort_kv(arriving, kv_received))
    for _ in range(BACK):
        block = after(lasts[-1], firsts[-1])
        firsts.append(along(firsts[-1], 1))
        lasts.append(along(block, 1))
    firsts[-1] = after(firsts[-1], lasts[-1])
    chains = [firsts[::-1], lasts[::-1]]

    results, totals, own = [], [], []
    for n in range(2):
        result, *parts = attend(meta, arriving, received[n], chains[n], counts[n], room=n)
        total = parts[0]
        for part in parts[1:-1]:
            total = (along(total, -1).astype(F32) + part).astype(BF16)
        totals.append(along(total, -1))
        own.append(parts[-1])
        results.append(result)

    back_first = exchange(results[0])
    merged = return_kv(arriving, *totals, *own, results[1])
    back_last = exchange(after(merged, back_first))

    outs = finish(leaving, q_gain, query, back_first, starts[0], counts[0])
    return tuple(
        finish(
            leaving,
            q_gain,
            query,
            back_last,
            starts[1],
            counts[1],
            kv=(k_gain, key_projection),
            earlier=outs,
        )
    )


def solution(mesh):
    rows = P(("dp", "seq"), None)
    in_specs = (rows, rows, rows, rows, P(), P(), P("dp", None)) + (P("dp", "seq", None),) * 2
    return jax.shard_map(
        per_device, mesh=mesh, in_specs=in_specs, out_specs=(rows,) * 4, check_vma=False
    )
```

```python
import functools

import jax
import jax.numpy as jnp
from jax import lax
from jax.experimental import pallas as pl
from jax.experimental.pallas import tpu as pltpu
from jax.sharding import PartitionSpec as P

Q_HEADS = 64
KV_HEADS = 8
HEAD = 128
RATIO = Q_HEADS // KV_HEADS
EPS = 1e-06
ROWS = 128
GROUPS = 32
SHARE = ROWS // GROUPS
SPLIT = 4
CHUNK = SHARE * SPLIT
TALL = GROUPS * CHUNK
WIDE = 2 * HEAD
BACK = 4
WINDOW = (BACK + 1) * ROWS
SCALE = HEAD ** (-0.5)
LOG2E = 1.4426950408889634
FIRST = 6
BATCHES = (3, 3, 2)
VMEM_LIMIT = 52 * 1024 * 1024
VMEM_WHOLE = 62 * 1024 * 1024
F32 = jnp.float32
BF16 = jnp.bfloat16


def params(limit=VMEM_LIMIT):
    return pltpu.CompilerParams(vmem_limit_bytes=limit)


def cost(flops, moved, trans=0):
    return pl.CostEstimate(flops=int(flops), bytes_accessed=int(moved), transcendentals=int(trans))


def dot(a, b, dims):
    return lax.dot_general(a, b, (dims, ((), ())), preferred_element_type=F32)


MM = ((1,), (0,))
MT = ((1,), (1,))
TM = ((0,), (0,))


def iota(shape, dim):
    return lax.broadcasted_iota(jnp.int32, shape, dim)


def tall_row(index):
    row = (index // CHUNK) * SHARE + index % SHARE
    part = (index // SHARE) % SPLIT
    return row, part


def home_matrix(order_ref):
    spread_row, _ = tall_row(iota((ROWS, TALL), 1))
    spread = (spread_row == iota((ROWS, TALL), 0)).astype(BF16)
    order = jnp.broadcast_to(order_ref[...].astype(F32), (16, ROWS)).astype(BF16)
    source = dot(order, spread, MM)[:1]
    _, part = tall_row(iota((1, TALL), 1))
    code = source + (part * ROWS).astype(F32)
    return (iota((TALL, TALL), 0).astype(F32) == code).astype(BF16)


def pack_matrix(order_ref):
    row, part = tall_row(iota((TALL, SPLIT * ROWS), 0))
    order = order_ref[...]
    code = jnp.concatenate([order + p * ROWS for p in range(SPLIT)], axis=1)
    return (row + part * ROWS == code).astype(BF16)


def norm(x, gain):
    factor = lax.rsqrt(jnp.mean(x * x, axis=-1, keepdims=True) + EPS)
    return x * factor * gain


def norm_back(x, gain, dy):
    factor = lax.rsqrt(jnp.mean(x * x, axis=-1, keepdims=True) + EPS)
    g = dy * gain
    inner = jnp.mean(x * g, axis=-1, keepdims=True)
    return factor * g - x * (factor * factor * factor * inner)


def head_cols(h):
    return slice(h * HEAD, (h + 1) * HEAD)


def send_kv_kernel(order_ref, gain_ref, k_ref, v_ref, out_ref):
    gain = gain_ref[...]
    kn = [
        norm(k_ref[:, head_cols(h)].astype(F32), gain).astype(BF16) for h in range(KV_HEADS)
    ]
    half = KV_HEADS * HEAD // 2
    stack = jnp.concatenate(
        [
            jnp.concatenate(kn[: KV_HEADS // 2], axis=1),
            jnp.concatenate(kn[KV_HEADS // 2 :], axis=1),
            v_ref[:, :half],
            v_ref[:, half:],
        ],
        axis=0,
    )
    sent = dot(home_matrix(order_ref), stack, TM).astype(BF16)
    out_ref[...] = sent.reshape(GROUPS, CHUNK, half)


def send_kv(order, gain, key_projection, value):
    half = KV_HEADS * HEAD // 2
    return pl.pallas_call(
        send_kv_kernel,
        out_shape=jax.ShapeDtypeStruct((GROUPS, CHUNK, half), BF16),
        compiler_params=params(VMEM_WHOLE),
        cost_estimate=cost(2 * TALL * TALL * half, 3 << 19),
        name="send_kv",
    )(order, gain, key_projection, value)


def send_rows_kernel(order_ref, gain_ref, q_ref, d_ref, out_ref, home_ref):
    @pl.when(pl.program_id(0) == 0)
    def _():
        home_ref[...] = home_matrix(order_ref)

    gain = gain_ref[...]
    qn = [norm(q_ref[:, head_cols(h)].astype(F32), gain).astype(BF16) for h in range(RATIO)]
    stack = jnp.concatenate(
        [
            jnp.concatenate(
                [qn[2 * p], qn[2 * p + 1], d_ref[:, p * WIDE : (p + 1) * WIDE]], axis=1
            )
            for p in range(SPLIT)
        ],
        axis=0,
    )
    sent = dot(home_ref[...], stack, TM).astype(BF16)
    out_ref[...] = sent.reshape(GROUPS, CHUNK, 2 * WIDE)


def send_rows(order, gain, query, d_out, first, count):
    return pl.pallas_call(
        send_rows_kernel,
        grid=(count,),
        in_specs=[
            pl.BlockSpec((1, ROWS), lambda h: (0, 0)),
            pl.BlockSpec((1, HEAD), lambda h: (0, 0)),
            pl.BlockSpec((ROWS, RATIO * HEAD), lambda h: (0, h + first)),
            pl.BlockSpec((ROWS, RATIO * HEAD), lambda h: (0, h + first)),
        ],
        out_specs=pl.BlockSpec((GROUPS, CHUNK, 2 * WIDE), lambda h: (0, 0, h)),
        out_shape=jax.ShapeDtypeStruct((GROUPS, CHUNK, count * 2 * WIDE), BF16),
        scratch_shapes=[pltpu.VMEM((TALL, TALL), BF16)],
        compiler_params=params(VMEM_WHOLE),
        cost_estimate=cost(count * 2 * TALL * TALL * 2 * WIDE, count << 20),
        name="send_rows",
    )(order, gain, query, d_out)


def sort_kv_kernel(order_ref, in_ref, *out_refs):
    half = KV_HEADS * HEAD // 2
    rows = dot(pack_matrix(order_ref), in_ref[...].reshape(TALL, half), TM).astype(BF16)
    places = [(ref, at) for ref, count in zip(out_refs, BATCHES) for at in range(count)]
    for h, (ref, at) in enumerate(places):
        part, cols = h // (KV_HEADS // 2), head_cols(h % (KV_HEADS // 2))
        k = rows[part * ROWS : (part + 1) * ROWS, cols]
        v = rows[(part + 2) * ROWS : (part + 3) * ROWS, cols]
        ref[:, at * WIDE : (at + 1) * WIDE] = jnp.concatenate([k, v], axis=1)


def sort_kv(order, received):
    return pl.pallas_call(
        sort_kv_kernel,
        out_shape=[jax.ShapeDtypeStruct((ROWS, count * WIDE), BF16) for count in BATCHES],
        compiler_params=params(),
        cost_estimate=cost(2 * TALL**3, 1 << 20),
        name="sort_kv",
    )(order, received)


def attend_kernel(meta_ref, order_ref, qd_ref, *refs):
    kv_refs = refs[: BACK + 1]
    out_ref, *part_refs, bias_ref = refs[-(BACK + 3) :]

    @pl.when(pl.program_id(0) == 0)
    def _():
        places = jnp.broadcast_to(iota((1, ROWS), 1).astype(F32), (16, ROWS)).astype(BF16)
        arrived = (iota((ROWS, ROWS), 0) == order_ref[...]).astype(BF16)
        place = dot(places, arrived, MT).astype(BF16)
        row, _ = tall_row(iota((ROWS, TALL), 1))
        spread = (row == iota((ROWS, TALL), 0)).astype(BF16)
        base = meta_ref[3] * ROWS
        position = dot(place, spread, MM)[:1] + base.astype(F32)
        end0 = meta_ref[0].astype(F32)
        end1 = (meta_ref[0] + meta_ref[1]).astype(F32)
        start = jnp.where(position < end0, 0.0, jnp.where(position < end1, end0, end1))
        key = (iota((WINDOW, TALL), 0) + (base - BACK * ROWS)).astype(F32)
        bias_ref[...] = jnp.where((key >= start) & (key <= position), 0.0, -1e30)

    kw = jnp.concatenate([r[:, :HEAD] for r in kv_refs], axis=0)
    vw = jnp.concatenate([r[:, HEAD:] for r in kv_refs], axis=0)

    def both(low):
        return jnp.concatenate(
            [
                qd_ref[:, :, low + e * HEAD : low + (e + 1) * HEAD].reshape(TALL, HEAD)
                for e in range(2)
            ],
            axis=0,
        )

    q, d = both(0), both(WIDE)
    scores = dot(kw, q, MT)
    d_weights = dot(vw, d, MT)
    bias = bias_ref[...]
    expo = jnp.exp2(scores * (SCALE * LOG2E) + jnp.concatenate([bias, bias], axis=1))
    weights = expo * (1.0 / jnp.sum(expo, axis=0, keepdims=True))
    low_weights = weights.astype(BF16)
    out = dot(vw, low_weights, TM).astype(BF16)
    delta = jnp.sum(d.astype(F32).T * out.astype(F32), axis=0, keepdims=True)
    d_scores = (weights * (d_weights - delta)).astype(BF16)
    dq = (dot(kw, d_scores, TM) * SCALE).astype(BF16)
    dk = dot(d_scores, q, MM) * SCALE
    dv = dot(low_weights, d, MM)
    for low, value in ((0, out.T), (WIDE, dq.T)):
        for e in range(2):
            out_ref[:, :, low + e * HEAD : low + (e + 1) * HEAD] = value[
                e * TALL : (e + 1) * TALL
            ].reshape(GROUPS, CHUNK, HEAD)
    for n, ref in enumerate(part_refs):
        ref[:, :HEAD] = dk[n * ROWS : (n + 1) * ROWS].astype(ref.dtype)
        ref[:, HEAD:] = dv[n * ROWS : (n + 1) * ROWS].astype(ref.dtype)


def attend(meta, order, received, blocks, first, count, result, weight):
    kv_spec = pl.BlockSpec((ROWS, WIDE), lambda h: (0, h))
    rows_spec = pl.BlockSpec((GROUPS, CHUNK, 2 * WIDE), lambda h: (0, 0, h + first))
    elements = count * RATIO * ROWS * WINDOW
    fresh = isinstance(result, int)
    shape = (GROUPS, CHUNK, result * 2 * WIDE) if fresh else result.shape
    return pl.pallas_call(
        attend_kernel,
        grid=(count,),
        in_specs=[
            pl.BlockSpec(memory_space=pltpu.SMEM),
            pl.BlockSpec((1, ROWS), lambda h: (0, 0)),
            rows_spec,
        ]
        + [kv_spec] * (BACK + 1)
        + ([] if fresh else [pl.BlockSpec(memory_space=pl.ANY)]),
        out_specs=[rows_spec] + [kv_spec] * (BACK + 1),
        out_shape=[jax.ShapeDtypeStruct(shape, BF16)]
        + [
            jax.ShapeDtypeStruct((ROWS, count * WIDE), BF16 if n == 0 else F32)
            for n in range(BACK + 1)
        ],
        scratch_shapes=[pltpu.VMEM((WINDOW, TALL), F32)],
        input_output_aliases={} if fresh else {BACK + 4: 0},
        compiler_params=params(),
        cost_estimate=cost(weight * elements * HEAD, count * (3 << 20), elements),
        name="attend",
    )(meta, order, received, *blocks, *(() if fresh else (result,)))


def return_kv_kernel(order_ref, *refs):
    half = KV_HEADS * HEAD // 2
    count, out_ref = len(BATCHES), refs[-1]
    total = jnp.concatenate(
        [
            (got[...].astype(F32) + own[...]).astype(BF16)
            for got, own in zip(refs[:count], refs[count : 2 * count])
        ],
        axis=1,
    )

    def columns(which, part):
        heads = range(part * KV_HEADS // 2, (part + 1) * KV_HEADS // 2)
        return jnp.concatenate([total[:, head_cols(2 * h + which)] for h in heads], axis=1)

    stack = jnp.concatenate(
        [columns(which, part) for which in range(2) for part in range(2)], axis=0
    )
    rows = dot(pack_matrix(order_ref), stack, MM).astype(BF16)
    out_ref[...] = rows.reshape(GROUPS, CHUNK, half)


def return_kv(order, got, own, result):
    half = KV_HEADS * HEAD // 2
    place = result.shape[2] // half - 1
    small = [pl.BlockSpec(a.shape, lambda i: (0, 0)) for a in (order, *got, *own)]
    return pl.pallas_call(
        return_kv_kernel,
        grid=(1,),
        in_specs=small + [pl.BlockSpec(memory_space=pl.ANY)],
        out_specs=pl.BlockSpec((GROUPS, CHUNK, half), lambda i: (0, 0, place)),
        out_shape=jax.ShapeDtypeStruct(result.shape, BF16),
        input_output_aliases={len(small): 0},
        compiler_params=params(),
        cost_estimate=cost(2 * TALL**3, 3 << 20),
        name="return_kv",
    )(order, *got, *own, result)


def finish_rows_step(rows, gain, q_ref, out_ref, dq_ref):
    for part in range(SPLIT):
        mine = rows[part * ROWS : (part + 1) * ROWS]
        out_ref[:, part * WIDE : (part + 1) * WIDE] = mine[:, :WIDE].astype(BF16)
        for e in range(2):
            at = head_cols(2 * part + e)
            dy = mine[:, WIDE + e * HEAD : WIDE + (e + 1) * HEAD]
            dq_ref[:, at] = norm_back(q_ref[:, at].astype(F32), gain, dy).astype(BF16)


def finish_kv_step(rows, gain, k_ref, dk_ref, dv_ref):
    half = KV_HEADS * HEAD // 2
    for h in range(KV_HEADS):
        part, cols = h // (KV_HEADS // 2), head_cols(h % (KV_HEADS // 2))
        dy = rows[part * ROWS : (part + 1) * ROWS, cols]
        dk_ref[:, head_cols(h)] = norm_back(
            k_ref[:, head_cols(h)].astype(F32), gain, dy
        ).astype(BF16)
    dv_ref[:, :half] = rows[2 * ROWS : 3 * ROWS].astype(BF16)
    dv_ref[:, half:] = rows[3 * ROWS :].astype(BF16)


def finish_kernel(with_kv, order_ref, gain_ref, q_ref, in_ref, *refs):
    home_ref = refs[-1]
    step = pl.program_id(0)

    @pl.when(step == 0)
    def _():
        home_ref[...] = home_matrix(order_ref)

    rows = dot(home_ref[...], in_ref[...].reshape(TALL, 2 * WIDE), MM)
    if with_kv:
        k_gain_ref, k_ref, _, _, out_ref, dq_ref, dk_ref, dv_ref = refs[:-1]
        last = pl.num_programs(0) - 1

        @pl.when(step < last)
        def _():
            finish_rows_step(rows, gain_ref[...], q_ref, out_ref, dq_ref)

        @pl.when(step == last)
        def _():
            finish_kv_step(rows, k_gain_ref[...], k_ref, dk_ref, dv_ref)
    else:
        out_ref, dq_ref = refs[:-1]
        finish_rows_step(rows, gain_ref[...], q_ref, out_ref, dq_ref)


def finish(order, gain, query, received, first, count, kv=(), earlier=()):
    block = pl.BlockSpec((ROWS, RATIO * HEAD), lambda h: (0, jnp.minimum(h, count - 1) + first))
    whole = jax.ShapeDtypeStruct((ROWS, Q_HEADS * HEAD), BF16)
    row = pl.BlockSpec((1, ROWS), lambda h: (0, 0))
    kv_block = pl.BlockSpec((ROWS, KV_HEADS * HEAD), lambda h: (0, 0))
    kv_whole = jax.ShapeDtypeStruct((ROWS, KV_HEADS * HEAD), BF16)
    in_specs = [row, row, block, pl.BlockSpec((GROUPS, CHUNK, 2 * WIDE), lambda h: (0, 0, h))]
    if kv:
        in_specs += [row, kv_block] + [pl.BlockSpec(memory_space=pl.ANY)] * 2
    return pl.pallas_call(
        functools.partial(finish_kernel, bool(kv)),
        grid=(count + 1 if kv else count,),
        in_specs=in_specs,
        out_specs=[block, block] + ([kv_block] * 2 if kv else []),
        out_shape=[whole, whole] + ([kv_whole] * 2 if kv else []),
        scratch_shapes=[pltpu.VMEM((TALL, TALL), BF16)],
        input_output_aliases={6: 0, 7: 1} if kv else {},
        compiler_params=params(),
        cost_estimate=cost(count * 2 * TALL * TALL * 2 * WIDE, count * (5 << 18)),
        name="finish",
    )(order, gain, query, received, *kv, *earlier)


def exchange(array):
    return lax.all_to_all(array, "dp", split_axis=0, concat_axis=0, tiled=True)


def along(array, step):
    count = lax.axis_size("seq")
    return lax.ppermute(array, "seq", [(i, (i + step) % count) for i in range(count)])


def after(array, other):
    return array if other is None else lax.optimization_barrier((array, other))[0]


def per_device(
    query, key_projection, value, d_out, q_gain, key_norm_gain, seq_lengths, send_order, recv_order
):
    leaving = send_order.reshape(1, ROWS)
    arriving = recv_order.reshape(1, ROWS)
    q_gain = q_gain.reshape(1, HEAD)
    k_gain = key_norm_gain.reshape(1, HEAD)
    place = lax.axis_index("seq").astype(jnp.int32)
    meta = jnp.concatenate([seq_lengths[0], place[None]])
    counts = (FIRST, KV_HEADS - FIRST)
    starts = (0, FIRST)

    kv_sent = send_kv(leaving, k_gain, key_projection, value)
    kv_received = exchange(kv_sent)
    sent = [
        send_rows(leaving, q_gain, query, d_out, first, count)
        for first, count in zip(starts, counts)
    ]
    kv_received, *sent = lax.optimization_barrier((kv_received, *sent))
    received_first = exchange(sent[0])

    first, second, third = ([block] for block in sort_kv(arriving, kv_received))
    for n in range(BACK):
        first.append(along(after(first[-1], second[n - 1] if n > 1 else None), 1))
        second.append(along(second[-1], 1))
    received_last = exchange(after(after(sent[1], received_first), first[BACK]))
    for n in range(BACK):
        block = after(third[-1], (first[BACK], None, received_last, None)[n])
        third.append(along(block, 1))
    second[-1] = after(second[-1], third[1])

    def back_along(parts):
        total = parts[0]
        for part in parts[1:-1]:
            total = (along(total, -1).astype(F32) + part).astype(BF16)
        return along(total, -1), parts[-1]

    def attend_batch(rows, blocks, first, count, result, weight):
        result, *parts = attend(
            meta, arriving, rows, blocks[::-1], first, count, result, weight
        )
        return result, *back_along(parts)

    result, got0, own0 = attend_batch(received_first, first, 0, BATCHES[0], FIRST, 4)
    result, got1, own1 = attend_batch(
        received_first, second, BATCHES[0], BATCHES[1], result, 36
    )
    back_first = exchange(result)
    result, got2, own2 = attend_batch(received_last, third, 0, BATCHES[2], BATCHES[2] + 1, 36)
    merged = return_kv(arriving, (got0, got1, got2), (own0, own1, own2), result)
    back_last = exchange(after(merged, back_first))

    outs = finish(leaving, q_gain, query, back_first, starts[0], counts[0])
    return tuple(
        finish(
            leaving,
            q_gain,
            query,
            back_last,
            starts[1],
            counts[1],
            kv=(k_gain, key_projection),
            earlier=outs,
        )
    )


def solution(mesh):
    rows = P(("dp", "seq"), None)
    in_specs = (rows, rows, rows, rows, P(), P(), P("dp", None)) + (P("dp", "seq", None),) * 2
    return jax.shard_map(
        per_device, mesh=mesh, in_specs=in_specs, out_specs=(rows,) * 4, check_vma=False
    )
```

```python
import functools

import jax
import jax.numpy as jnp
from jax import lax
from jax.experimental import pallas as pl
from jax.experimental.pallas import tpu as pltpu
from jax.sharding import PartitionSpec as P

Q_HEADS = 64
KV_HEADS = 8
HEAD = 128
RATIO = Q_HEADS // KV_HEADS
EPS = 1e-06
ROWS = 128
GROUPS = 32
SHARE = ROWS // GROUPS
SPLIT = 4
CHUNK = SHARE * SPLIT
TALL = GROUPS * CHUNK
WIDE = 2 * HEAD
BACK = 4
WINDOW = (BACK + 1) * ROWS
SCALE = HEAD ** (-0.5)
LOG2E = 1.4426950408889634
FIRST = 6
BATCHES = (3, 3, 2)
VMEM_LIMIT = 52 * 1024 * 1024
VMEM_WHOLE = 62 * 1024 * 1024
F32 = jnp.float32
BF16 = jnp.bfloat16


def params(limit=VMEM_LIMIT):
    return pltpu.CompilerParams(vmem_limit_bytes=limit)


def cost(flops, moved, trans=0):
    return pl.CostEstimate(flops=int(flops), bytes_accessed=int(moved), transcendentals=int(trans))


def dot(a, b, dims):
    return lax.dot_general(a, b, (dims, ((), ())), preferred_element_type=F32)


MM = ((1,), (0,))
MT = ((1,), (1,))
TM = ((0,), (0,))


def iota(shape, dim):
    return lax.broadcasted_iota(jnp.int32, shape, dim)


def tall_row(index):
    row = (index // CHUNK) * SHARE + index % SHARE
    part = (index // SHARE) % SPLIT
    return row, part


def home_matrix(order_ref):
    spread_row, _ = tall_row(iota((ROWS, TALL), 1))
    spread = (spread_row == iota((ROWS, TALL), 0)).astype(BF16)
    order = jnp.broadcast_to(order_ref[...].astype(F32), (16, ROWS)).astype(BF16)
    source = dot(order, spread, MM)[:1]
    _, part = tall_row(iota((1, TALL), 1))
    code = source + (part * ROWS).astype(F32)
    return (iota((TALL, TALL), 0).astype(F32) == code).astype(BF16)


def pack_matrix(order_ref):
    row, part = tall_row(iota((TALL, SPLIT * ROWS), 0))
    order = order_ref[...]
    code = jnp.concatenate([order + p * ROWS for p in range(SPLIT)], axis=1)
    return (row + part * ROWS == code).astype(BF16)


def norm(x, gain):
    factor = lax.rsqrt(jnp.mean(x * x, axis=-1, keepdims=True) + EPS)
    return x * factor * gain


def norm_back(x, gain, dy):
    factor = lax.rsqrt(jnp.mean(x * x, axis=-1, keepdims=True) + EPS)
    g = dy * gain
    inner = jnp.mean(x * g, axis=-1, keepdims=True)
    return factor * g - x * (factor * factor * factor * inner)


def head_cols(h):
    return slice(h * HEAD, (h + 1) * HEAD)


def send_kv_kernel(order_ref, gain_ref, k_ref, v_ref, out_ref):
    gain = gain_ref[...]
    kn = [
        norm(k_ref[:, head_cols(h)].astype(F32), gain).astype(BF16) for h in range(KV_HEADS)
    ]
    half = KV_HEADS * HEAD // 2
    stack = jnp.concatenate(
        [
            jnp.concatenate(kn[: KV_HEADS // 2], axis=1),
            jnp.concatenate(kn[KV_HEADS // 2 :], axis=1),
            v_ref[:, :half],
            v_ref[:, half:],
        ],
        axis=0,
    )
    sent = dot(home_matrix(order_ref), stack, TM).astype(BF16)
    out_ref[...] = sent.reshape(GROUPS, CHUNK, half)


def send_kv(order, gain, key_projection, value):
    half = KV_HEADS * HEAD // 2
    return pl.pallas_call(
        send_kv_kernel,
        out_shape=jax.ShapeDtypeStruct((GROUPS, CHUNK, half), BF16),
        compiler_params=params(VMEM_WHOLE),
        cost_estimate=cost(2 * TALL * TALL * half, 3 << 19),
        name="send_kv",
    )(order, gain, key_projection, value)


def send_rows_kernel(order_ref, gain_ref, q_ref, d_ref, out_ref, home_ref):
    @pl.when(pl.program_id(0) == 0)
    def _():
        home_ref[...] = home_matrix(order_ref)

    gain = gain_ref[...]
    qn = [norm(q_ref[:, head_cols(h)].astype(F32), gain).astype(BF16) for h in range(RATIO)]
    stack = jnp.concatenate(
        [
            jnp.concatenate(
                [qn[2 * p], qn[2 * p + 1], d_ref[:, p * WIDE : (p + 1) * WIDE]], axis=1
            )
            for p in range(SPLIT)
        ],
        axis=0,
    )
    sent = dot(home_ref[...], stack, TM).astype(BF16)
    out_ref[...] = sent.reshape(GROUPS, CHUNK, 2 * WIDE)


def send_rows(order, gain, query, d_out, first, count):
    return pl.pallas_call(
        send_rows_kernel,
        grid=(count,),
        in_specs=[
            pl.BlockSpec((1, ROWS), lambda h: (0, 0)),
            pl.BlockSpec((1, HEAD), lambda h: (0, 0)),
            pl.BlockSpec((ROWS, RATIO * HEAD), lambda h: (0, h + first)),
            pl.BlockSpec((ROWS, RATIO * HEAD), lambda h: (0, h + first)),
        ],
        out_specs=pl.BlockSpec((GROUPS, CHUNK, 2 * WIDE), lambda h: (0, 0, h)),
        out_shape=jax.ShapeDtypeStruct((GROUPS, CHUNK, count * 2 * WIDE), BF16),
        scratch_shapes=[pltpu.VMEM((TALL, TALL), BF16)],
        compiler_params=params(VMEM_WHOLE),
        cost_estimate=cost(count * 2 * TALL * TALL * 2 * WIDE, count << 20),
        name="send_rows",
    )(order, gain, query, d_out)


def sort_kv_kernel(order_ref, in_ref, *out_refs):
    half = KV_HEADS * HEAD // 2
    rows = dot(pack_matrix(order_ref), in_ref[...].reshape(TALL, half), TM).astype(BF16)
    places = [(ref, at) for ref, count in zip(out_refs, BATCHES) for at in range(count)]
    for h, (ref, at) in enumerate(places):
        part, cols = h // (KV_HEADS // 2), head_cols(h % (KV_HEADS // 2))
        k = rows[part * ROWS : (part + 1) * ROWS, cols]
        v = rows[(part + 2) * ROWS : (part + 3) * ROWS, cols]
        ref[:, at * WIDE : (at + 1) * WIDE] = jnp.concatenate([k, v], axis=1)


def sort_kv(order, received):
    return pl.pallas_call(
        sort_kv_kernel,
        out_shape=[jax.ShapeDtypeStruct((ROWS, count * WIDE), BF16) for count in BATCHES],
        compiler_params=params(),
        cost_estimate=cost(2 * TALL**3, 1 << 20),
        name="sort_kv",
    )(order, received)


def attend_kernel(meta_ref, order_ref, qd_ref, *refs):
    kv_refs = refs[: BACK + 1]
    out_ref, *part_refs, bias_ref = refs[-(BACK + 3) :]

    @pl.when(pl.program_id(0) == 0)
    def _():
        places = jnp.broadcast_to(iota((1, ROWS), 1).astype(F32), (16, ROWS)).astype(BF16)
        arrived = (iota((ROWS, ROWS), 0) == order_ref[...]).astype(BF16)
        place = dot(places, arrived, MT).astype(BF16)
        row, _ = tall_row(iota((ROWS, TALL), 1))
        spread = (row == iota((ROWS, TALL), 0)).astype(BF16)
        base = meta_ref[3] * ROWS
        position = dot(place, spread, MM)[:1] + base.astype(F32)
        end0 = meta_ref[0].astype(F32)
        end1 = (meta_ref[0] + meta_ref[1]).astype(F32)
        start = jnp.where(position < end0, 0.0, jnp.where(position < end1, end0, end1))
        key = (iota((WINDOW, TALL), 0) + (base - BACK * ROWS)).astype(F32)
        bias_ref[...] = jnp.where((key >= start) & (key <= position), 0.0, -1e30)

    kw = jnp.concatenate([r[:, :HEAD] for r in kv_refs], axis=0)
    vw = jnp.concatenate([r[:, HEAD:] for r in kv_refs], axis=0)

    def both(low):
        return jnp.concatenate(
            [
                qd_ref[:, :, low + e * HEAD : low + (e + 1) * HEAD].reshape(TALL, HEAD)
                for e in range(2)
            ],
            axis=0,
        )

    q, d = both(0), both(WIDE)
    scores = dot(kw, q, MT)
    d_weights = dot(vw, d, MT)
    bias = bias_ref[...]
    expo = jnp.exp2(scores * (SCALE * LOG2E) + jnp.concatenate([bias, bias], axis=1))
    weights = expo * (1.0 / jnp.sum(expo, axis=0, keepdims=True))
    low_weights = weights.astype(BF16)
    out = dot(vw, low_weights, TM).astype(BF16)
    delta = jnp.sum(d.astype(F32).T * out.astype(F32), axis=0, keepdims=True)
    d_scores = (weights * (d_weights - delta)).astype(BF16)
    dq = (dot(kw, d_scores, TM) * SCALE).astype(BF16)
    dk = dot(d_scores, q, MM) * SCALE
    dv = dot(low_weights, d, MM)
    for low, value in ((0, out.T), (WIDE, dq.T)):
        for e in range(2):
            out_ref[:, :, low + e * HEAD : low + (e + 1) * HEAD] = value[
                e * TALL : (e + 1) * TALL
            ].reshape(GROUPS, CHUNK, HEAD)
    for n, ref in enumerate(part_refs):
        ref[:, :HEAD] = dk[n * ROWS : (n + 1) * ROWS].astype(ref.dtype)
        ref[:, HEAD:] = dv[n * ROWS : (n + 1) * ROWS].astype(ref.dtype)


def attend(meta, order, received, blocks, first, count, result, weight):
    kv_spec = pl.BlockSpec((ROWS, WIDE), lambda h: (0, h))
    rows_spec = pl.BlockSpec((GROUPS, CHUNK, 2 * WIDE), lambda h: (0, 0, h + first))
    elements = count * RATIO * ROWS * WINDOW
    fresh = isinstance(result, int)
    shape = (GROUPS, CHUNK, result * 2 * WIDE) if fresh else result.shape
    return pl.pallas_call(
        attend_kernel,
        grid=(count,),
        in_specs=[
            pl.BlockSpec(memory_space=pltpu.SMEM),
            pl.BlockSpec((1, ROWS), lambda h: (0, 0)),
            rows_spec,
        ]
        + [kv_spec] * (BACK + 1)
        + ([] if fresh else [pl.BlockSpec(memory_space=pl.ANY)]),
        out_specs=[rows_spec] + [kv_spec] * (BACK + 1),
        out_shape=[jax.ShapeDtypeStruct(shape, BF16)]
        + [
            jax.ShapeDtypeStruct((ROWS, count * WIDE), BF16 if n == 0 else F32)
            for n in range(BACK + 1)
        ],
        scratch_shapes=[pltpu.VMEM((WINDOW, TALL), F32)],
        input_output_aliases={} if fresh else {BACK + 4: 0},
        compiler_params=params(),
        cost_estimate=cost(weight * elements * HEAD, count * (3 << 20), elements),
        name="attend",
    )(meta, order, received, *blocks, *(() if fresh else (result,)))


def return_kv_kernel(order_ref, *refs):
    half = KV_HEADS * HEAD // 2
    count, out_ref = len(BATCHES), refs[-1]
    total = jnp.concatenate(
        [
            (got[...].astype(F32) + own[...]).astype(BF16)
            for got, own in zip(refs[:count], refs[count : 2 * count])
        ],
        axis=1,
    )

    def columns(which, part):
        heads = range(part * KV_HEADS // 2, (part + 1) * KV_HEADS // 2)
        return jnp.concatenate([total[:, head_cols(2 * h + which)] for h in heads], axis=1)

    stack = jnp.concatenate(
        [columns(which, part) for which in range(2) for part in range(2)], axis=0
    )
    rows = dot(pack_matrix(order_ref), stack, MM).astype(BF16)
    out_ref[...] = rows.reshape(GROUPS, CHUNK, half)


def return_kv(order, got, own, result):
    half = KV_HEADS * HEAD // 2
    place = result.shape[2] // half - 1
    small = [pl.BlockSpec(a.shape, lambda i: (0, 0)) for a in (order, *got, *own)]
    return pl.pallas_call(
        return_kv_kernel,
        grid=(1,),
        in_specs=small + [pl.BlockSpec(memory_space=pl.ANY)],
        out_specs=pl.BlockSpec((GROUPS, CHUNK, half), lambda i: (0, 0, place)),
        out_shape=jax.ShapeDtypeStruct(result.shape, BF16),
        input_output_aliases={len(small): 0},
        compiler_params=params(),
        cost_estimate=cost(2 * TALL**3, 3 << 20),
        name="return_kv",
    )(order, *got, *own, result)


def finish_rows_step(rows, gain, q_ref, out_ref, dq_ref):
    for part in range(SPLIT):
        mine = rows[part * ROWS : (part + 1) * ROWS]
        out_ref[:, part * WIDE : (part + 1) * WIDE] = mine[:, :WIDE].astype(BF16)
        for e in range(2):
            at = head_cols(2 * part + e)
            dy = mine[:, WIDE + e * HEAD : WIDE + (e + 1) * HEAD]
            dq_ref[:, at] = norm_back(q_ref[:, at].astype(F32), gain, dy).astype(BF16)


def finish_kv_step(rows, gain, k_ref, dk_ref, dv_ref):
    half = KV_HEADS * HEAD // 2
    for h in range(KV_HEADS):
        part, cols = h // (KV_HEADS // 2), head_cols(h % (KV_HEADS // 2))
        dy = rows[part * ROWS : (part + 1) * ROWS, cols]
        dk_ref[:, head_cols(h)] = norm_back(
            k_ref[:, head_cols(h)].astype(F32), gain, dy
        ).astype(BF16)
    dv_ref[:, :half] = rows[2 * ROWS : 3 * ROWS].astype(BF16)
    dv_ref[:, half:] = rows[3 * ROWS :].astype(BF16)


def finish_kernel(with_kv, order_ref, gain_ref, q_ref, in_ref, *refs):
    home_ref = refs[-1]
    step = pl.program_id(0)

    @pl.when(step == 0)
    def _():
        home_ref[...] = home_matrix(order_ref)

    rows = dot(home_ref[...], in_ref[...].reshape(TALL, 2 * WIDE), MM)
    if with_kv:
        k_gain_ref, k_ref, _, _, out_ref, dq_ref, dk_ref, dv_ref = refs[:-1]
        last = pl.num_programs(0) - 1

        @pl.when(step < last)
        def _():
            finish_rows_step(rows, gain_ref[...], q_ref, out_ref, dq_ref)

        @pl.when(step == last)
        def _():
            finish_kv_step(rows, k_gain_ref[...], k_ref, dk_ref, dv_ref)
    else:
        out_ref, dq_ref = refs[:-1]
        finish_rows_step(rows, gain_ref[...], q_ref, out_ref, dq_ref)


def finish(order, gain, query, received, first, count, kv=(), earlier=()):
    block = pl.BlockSpec((ROWS, RATIO * HEAD), lambda h: (0, jnp.minimum(h, count - 1) + first))
    whole = jax.ShapeDtypeStruct((ROWS, Q_HEADS * HEAD), BF16)
    row = pl.BlockSpec((1, ROWS), lambda h: (0, 0))
    kv_block = pl.BlockSpec((ROWS, KV_HEADS * HEAD), lambda h: (0, 0))
    kv_whole = jax.ShapeDtypeStruct((ROWS, KV_HEADS * HEAD), BF16)
    in_specs = [row, row, block, pl.BlockSpec((GROUPS, CHUNK, 2 * WIDE), lambda h: (0, 0, h))]
    if kv:
        in_specs += [row, kv_block] + [pl.BlockSpec(memory_space=pl.ANY)] * 2
    return pl.pallas_call(
        functools.partial(finish_kernel, bool(kv)),
        grid=(count + 1 if kv else count,),
        in_specs=in_specs,
        out_specs=[block, block] + ([kv_block] * 2 if kv else []),
        out_shape=[whole, whole] + ([kv_whole] * 2 if kv else []),
        scratch_shapes=[pltpu.VMEM((TALL, TALL), BF16)],
        input_output_aliases={6: 0, 7: 1} if kv else {},
        compiler_params=params(),
        cost_estimate=cost(count * 2 * TALL * TALL * 2 * WIDE, count * (5 << 18)),
        name="finish",
    )(order, gain, query, received, *kv, *earlier)


def exchange(array):
    return lax.all_to_all(array, "dp", split_axis=0, concat_axis=0, tiled=True)


def along(array, step):
    count = lax.axis_size("seq")
    pairs = [(i, i + step) for i in range(count) if 0 <= i + step < count]
    return lax.ppermute(array, "seq", pairs)


def after(array, other):
    return array if other is None else lax.optimization_barrier((array, other))[0]


def per_device(
    query, key_projection, value, d_out, q_gain, key_norm_gain, seq_lengths, send_order, recv_order
):
    leaving = send_order.reshape(1, ROWS)
    arriving = recv_order.reshape(1, ROWS)
    q_gain = q_gain.reshape(1, HEAD)
    k_gain = key_norm_gain.reshape(1, HEAD)
    place = lax.axis_index("seq").astype(jnp.int32)
    meta = jnp.concatenate([seq_lengths[0], place[None]])
    counts = (FIRST, KV_HEADS - FIRST)
    starts = (0, FIRST)

    kv_sent = send_kv(leaving, k_gain, key_projection, value)
    kv_received = exchange(kv_sent)
    sent = [
        send_rows(leaving, q_gain, query, d_out, first, count)
        for first, count in zip(starts, counts)
    ]
    kv_received, *sent = lax.optimization_barrier((kv_received, *sent))
    received_first = exchange(sent[0])

    first, second, third = ([block] for block in sort_kv(arriving, kv_received))
    for n in range(BACK):
        first.append(along(after(first[-1], second[n - 1] if n > 1 else None), 1))
        second.append(along(second[-1], 1))
    received_last = exchange(after(after(sent[1], received_first), first[BACK]))
    third[0] = after(third[0], first[BACK])
    for _ in range(BACK):
        third.append(along(third[-1], 1))
    second[-1] = after(second[-1], third[2])

    def back_along(parts):
        totals = parts[:1]
        for part in parts[1:-1]:
            totals.append((along(totals[-1], -1).astype(F32) + part).astype(BF16))
        return totals + [along(totals[-1], -1)], parts[-1]

    def attend_batch(rows, blocks, first, count, result, weight):
        result, *parts = attend(
            meta, arriving, rows, blocks[::-1], first, count, result, weight
        )
        return result, *back_along(parts)

    result, sums0, own0 = attend_batch(received_first, first, 0, BATCHES[0], FIRST, 1)
    result, sums1, own1 = attend_batch(
        received_first, second, BATCHES[0], BATCHES[1], result, 24
    )
    back_first = exchange(after(after(result, third[3]), sums0[1]))
    third[-1] = after(third[-1], sums0[2])
    result, sums2, own2 = attend_batch(received_last, third, 0, BATCHES[2], BATCHES[2] + 1, 36)
    merged = return_kv(arriving, (sums0[-1], sums1[-1], sums2[-1]), (own0, own1, own2), result)
    back_last = exchange(after(merged, back_first))

    outs = finish(leaving, q_gain, query, back_first, starts[0], counts[0])
    return tuple(
        finish(
            leaving,
            q_gain,
            query,
            back_last,
            starts[1],
            counts[1],
            kv=(k_gain, key_projection),
            earlier=outs,
        )
    )


def solution(mesh):
    rows = P(("dp", "seq"), None)
    in_specs = (rows, rows, rows, rows, P(), P(), P("dp", None)) + (P("dp", "seq", None),) * 2
    return jax.shard_map(
        per_device, mesh=mesh, in_specs=in_specs, out_specs=(rows,) * 4, check_vma=False
    )
```

```python
import functools

import jax
import jax.numpy as jnp
from jax import lax
from jax.experimental import pallas as pl
from jax.experimental.pallas import tpu as pltpu
from jax.sharding import PartitionSpec as P

Q_HEADS = 64
KV_HEADS = 8
HEAD = 128
RATIO = Q_HEADS // KV_HEADS
EPS = 1e-06
ROWS = 128
GROUPS = 32
SHARE = ROWS // GROUPS
SPLIT = 4
CHUNK = SHARE * SPLIT
TALL = GROUPS * CHUNK
WIDE = 2 * HEAD
BACK = 4
WINDOW = (BACK + 1) * ROWS
SCALE = HEAD ** (-0.5)
LOG2E = 1.4426950408889634
SMALL = 2
LARGE = KV_HEADS - SMALL
WEIGHTS = (36, 36)
VMEM_LIMIT = 52 * 1024 * 1024
VMEM_WHOLE = 62 * 1024 * 1024
F32 = jnp.float32
BF16 = jnp.bfloat16


def params(limit=VMEM_LIMIT):
    return pltpu.CompilerParams(vmem_limit_bytes=limit)


def cost(flops, moved, trans=0):
    return pl.CostEstimate(flops=int(flops), bytes_accessed=int(moved), transcendentals=int(trans))


def dot(a, b, dims):
    return lax.dot_general(a, b, (dims, ((), ())), preferred_element_type=F32)


MM = ((1,), (0,))
MT = ((1,), (1,))
TM = ((0,), (0,))


def iota(shape, dim):
    return lax.broadcasted_iota(jnp.int32, shape, dim)


def tall_row(index):
    row = (index // CHUNK) * SHARE + index % SHARE
    part = (index // SHARE) % SPLIT
    return row, part


def home_matrix(order_ref):
    spread_row, _ = tall_row(iota((ROWS, TALL), 1))
    spread = (spread_row == iota((ROWS, TALL), 0)).astype(BF16)
    order = jnp.broadcast_to(order_ref[...].astype(F32), (16, ROWS)).astype(BF16)
    source = dot(order, spread, MM)[:1]
    _, part = tall_row(iota((1, TALL), 1))
    code = source + (part * ROWS).astype(F32)
    return (iota((TALL, TALL), 0).astype(F32) == code).astype(BF16)


def pack_matrix(order_ref):
    row, part = tall_row(iota((TALL, SPLIT * ROWS), 0))
    order = order_ref[...]
    code = jnp.concatenate([order + p * ROWS for p in range(SPLIT)], axis=1)
    return (row + part * ROWS == code).astype(BF16)


def norm(x, gain):
    factor = lax.rsqrt(jnp.mean(x * x, axis=-1, keepdims=True) + EPS)
    return x * factor * gain


def norm_back(x, gain, dy):
    factor = lax.rsqrt(jnp.mean(x * x, axis=-1, keepdims=True) + EPS)
    g = dy * gain
    inner = jnp.mean(x * g, axis=-1, keepdims=True)
    return factor * g - x * (factor * factor * factor * inner)


def head_cols(h):
    return slice(h * HEAD, (h + 1) * HEAD)


def send_rows_step(home, gain, q_ref, d_ref):
    qn = [norm(q_ref[:, head_cols(h)].astype(F32), gain).astype(BF16) for h in range(RATIO)]
    stack = jnp.concatenate(
        [
            jnp.concatenate(
                [qn[2 * p], qn[2 * p + 1], d_ref[:, p * WIDE : (p + 1) * WIDE]], axis=1
            )
            for p in range(SPLIT)
        ],
        axis=0,
    )
    return dot(home, stack, TM).astype(BF16)


def send_kv_step(home, gain, k_ref, v_ref):
    kn = [
        norm(k_ref[:, head_cols(h)].astype(F32), gain).astype(BF16) for h in range(KV_HEADS)
    ]
    half = KV_HEADS * HEAD // 2
    stack = jnp.concatenate(
        [
            jnp.concatenate(kn[: KV_HEADS // 2], axis=1),
            jnp.concatenate(kn[KV_HEADS // 2 :], axis=1),
            v_ref[:, :half],
            v_ref[:, half:],
        ],
        axis=0,
    )
    return dot(home, stack, TM).astype(BF16)


def send_kernel(with_kv, order_ref, gain_ref, q_ref, d_ref, *refs):
    *kv_refs, out_ref, home_ref = refs
    step = pl.program_id(0)

    @pl.when(step == 0)
    def _():
        home_ref[...] = home_matrix(order_ref)

    def rows():
        sent = send_rows_step(home_ref[...], gain_ref[...], q_ref, d_ref)
        out_ref[...] = sent.reshape(out_ref.shape)

    if not with_kv:
        rows()
        return
    last = pl.num_programs(0) - 1
    pl.when(step < last)(rows)

    @pl.when(step == last)
    def _():
        gain, k_ref, v_ref = kv_refs
        sent = send_kv_step(home_ref[...], gain[...], k_ref, v_ref)
        out_ref[...] = sent.reshape(out_ref.shape)


def send(order, gain, query, d_out, first, count, kv=()):
    row = pl.BlockSpec((1, ROWS), lambda h: (0, 0))
    block = pl.BlockSpec((ROWS, RATIO * HEAD), lambda h: (0, jnp.minimum(h, count - 1) + first))
    kv_block = pl.BlockSpec((ROWS, KV_HEADS * HEAD), lambda h: (0, 0))
    parts = count + 1 if kv else count
    return pl.pallas_call(
        functools.partial(send_kernel, bool(kv)),
        grid=(parts,),
        in_specs=[row, row, block, block] + ([row, kv_block, kv_block] if kv else []),
        out_specs=pl.BlockSpec((GROUPS, CHUNK, 2 * WIDE), lambda h: (0, 0, h)),
        out_shape=jax.ShapeDtypeStruct((GROUPS, CHUNK, parts * 2 * WIDE), BF16),
        scratch_shapes=[pltpu.VMEM((TALL, TALL), BF16)],
        compiler_params=params(VMEM_WHOLE),
        cost_estimate=cost(parts * 2 * TALL * TALL * 2 * WIDE, parts << 20),
        name="send",
    )(order, gain, query, d_out, *kv)


def sort_kv_kernel(order_ref, in_ref, *out_refs):
    half = KV_HEADS * HEAD // 2
    rows = dot(pack_matrix(order_ref), in_ref[...].reshape(TALL, half), TM).astype(BF16)
    counts = (SMALL, LARGE)
    places = [(ref, at) for ref, count in zip(out_refs, counts) for at in range(count)]
    for h, (ref, at) in enumerate(places):
        part, cols = h // (KV_HEADS // 2), head_cols(h % (KV_HEADS // 2))
        k = rows[part * ROWS : (part + 1) * ROWS, cols]
        v = rows[(part + 2) * ROWS : (part + 3) * ROWS, cols]
        ref[:, at * WIDE : (at + 1) * WIDE] = jnp.concatenate([k, v], axis=1)


def sort_kv(order, received):
    return pl.pallas_call(
        sort_kv_kernel,
        grid=(1,),
        in_specs=[
            pl.BlockSpec((1, ROWS), lambda i: (0, 0)),
            pl.BlockSpec((GROUPS, CHUNK, 2 * WIDE), lambda i: (0, 0, SMALL)),
        ],
        out_specs=[
            pl.BlockSpec((ROWS, count * WIDE), lambda i: (0, 0)) for count in (SMALL, LARGE)
        ],
        out_shape=[
            jax.ShapeDtypeStruct((ROWS, count * WIDE), BF16) for count in (SMALL, LARGE)
        ],
        compiler_params=params(),
        cost_estimate=cost(2 * TALL**3, 1 << 20),
        name="sort_kv",
    )(order, received)


def attend_kernel(meta_ref, order_ref, qd_ref, *refs):
    kv_refs = refs[: BACK + 1]
    out_ref, *part_refs, bias_ref = refs[-(BACK + 3) :]

    @pl.when(pl.program_id(0) == 0)
    def _():
        places = jnp.broadcast_to(iota((1, ROWS), 1).astype(F32), (16, ROWS)).astype(BF16)
        arrived = (iota((ROWS, ROWS), 0) == order_ref[...]).astype(BF16)
        place = dot(places, arrived, MT).astype(BF16)
        row, _ = tall_row(iota((ROWS, TALL), 1))
        spread = (row == iota((ROWS, TALL), 0)).astype(BF16)
        base = meta_ref[3] * ROWS
        position = dot(place, spread, MM)[:1] + base.astype(F32)
        end0 = meta_ref[0].astype(F32)
        end1 = (meta_ref[0] + meta_ref[1]).astype(F32)
        start = jnp.where(position < end0, 0.0, jnp.where(position < end1, end0, end1))
        key = (iota((WINDOW, TALL), 0) + (base - BACK * ROWS)).astype(F32)
        bias_ref[...] = jnp.where((key >= start) & (key <= position), 0.0, -1e30)

    kw = jnp.concatenate([r[:, :HEAD] for r in kv_refs], axis=0)
    vw = jnp.concatenate([r[:, HEAD:] for r in kv_refs], axis=0)

    def both(low):
        return jnp.concatenate(
            [
                qd_ref[:, :, low + e * HEAD : low + (e + 1) * HEAD].reshape(TALL, HEAD)
                for e in range(2)
            ],
            axis=0,
        )

    q, d = both(0), both(WIDE)
    scores = dot(kw, q, MT)
    d_weights = dot(vw, d, MT)
    bias = bias_ref[...]
    expo = jnp.exp2(scores * (SCALE * LOG2E) + jnp.concatenate([bias, bias], axis=1))
    weights = expo * (1.0 / jnp.sum(expo, axis=0, keepdims=True))
    low_weights = weights.astype(BF16)
    out = dot(vw, low_weights, TM).astype(BF16)
    delta = jnp.sum(d.astype(F32).T * out.astype(F32), axis=0, keepdims=True)
    d_scores = (weights * (d_weights - delta)).astype(BF16)
    dq = (dot(kw, d_scores, TM) * SCALE).astype(BF16)
    dk = dot(d_scores, q, MM) * SCALE
    dv = dot(low_weights, d, MM)
    for low, value in ((0, out.T), (WIDE, dq.T)):
        for e in range(2):
            out_ref[:, :, low + e * HEAD : low + (e + 1) * HEAD] = value[
                e * TALL : (e + 1) * TALL
            ].reshape(GROUPS, CHUNK, HEAD)
    for n, ref in enumerate(part_refs):
        ref[:, :HEAD] = dk[n * ROWS : (n + 1) * ROWS].astype(ref.dtype)
        ref[:, HEAD:] = dv[n * ROWS : (n + 1) * ROWS].astype(ref.dtype)


def attend(meta, order, received, blocks, count, weight):
    kv_spec = pl.BlockSpec((ROWS, WIDE), lambda h: (0, h))
    rows_spec = pl.BlockSpec((GROUPS, CHUNK, 2 * WIDE), lambda h: (0, 0, h))
    elements = count * RATIO * ROWS * WINDOW
    return pl.pallas_call(
        attend_kernel,
        grid=(count,),
        in_specs=[
            pl.BlockSpec(memory_space=pltpu.SMEM),
            pl.BlockSpec((1, ROWS), lambda h: (0, 0)),
            rows_spec,
        ]
        + [kv_spec] * (BACK + 1),
        out_specs=[rows_spec] + [kv_spec] * (BACK + 1),
        out_shape=[jax.ShapeDtypeStruct((GROUPS, CHUNK, count * 2 * WIDE), BF16)]
        + [
            jax.ShapeDtypeStruct((ROWS, count * WIDE), BF16 if n == 0 else F32)
            for n in range(BACK + 1)
        ],
        scratch_shapes=[pltpu.VMEM((WINDOW, TALL), F32)],
        compiler_params=params(),
        cost_estimate=cost(weight * elements * HEAD, count * (3 << 20), elements),
        name="attend",
    )(meta, order, received, *blocks)


def return_kv_kernel(order_ref, *refs):
    half = KV_HEADS * HEAD // 2
    count, out_ref = len(refs) // 2, refs[-1]
    total = jnp.concatenate(
        [
            (got[...].astype(F32) + own[...]).astype(BF16)
            for got, own in zip(refs[:count], refs[count : 2 * count])
        ],
        axis=1,
    )

    def columns(which, part):
        heads = range(part * KV_HEADS // 2, (part + 1) * KV_HEADS // 2)
        return jnp.concatenate([total[:, head_cols(2 * h + which)] for h in heads], axis=1)

    stack = jnp.concatenate(
        [columns(which, part) for which in range(2) for part in range(2)], axis=0
    )
    rows = dot(pack_matrix(order_ref), stack, MM).astype(BF16)
    out_ref[...] = rows.reshape(GROUPS, CHUNK, half)


def return_kv(order, got, own):
    half = KV_HEADS * HEAD // 2
    return pl.pallas_call(
        return_kv_kernel,
        out_shape=jax.ShapeDtypeStruct((GROUPS, CHUNK, half), BF16),
        compiler_params=params(),
        cost_estimate=cost(2 * TALL**3, 3 << 20),
        name="return_kv",
    )(order, *got, *own)


def finish_rows_step(rows, gain, q_ref, out_ref, dq_ref):
    for part in range(SPLIT):
        mine = rows[part * ROWS : (part + 1) * ROWS]
        out_ref[:, part * WIDE : (part + 1) * WIDE] = mine[:, :WIDE].astype(BF16)
        for e in range(2):
            at = head_cols(2 * part + e)
            dy = mine[:, WIDE + e * HEAD : WIDE + (e + 1) * HEAD]
            dq_ref[:, at] = norm_back(q_ref[:, at].astype(F32), gain, dy).astype(BF16)


def finish_rows_kernel(order_ref, gain_ref, q_ref, in_ref, *refs):
    out_ref, dq_ref, home_ref = refs[-3:]

    @pl.when(pl.program_id(0) == 0)
    def _():
        home_ref[...] = home_matrix(order_ref)

    rows = dot(home_ref[...], in_ref[...].reshape(TALL, 2 * WIDE), MM)
    finish_rows_step(rows, gain_ref[...], q_ref, out_ref, dq_ref)


def finish_rows(order, gain, query, received, first, count, earlier=()):
    block = pl.BlockSpec((ROWS, RATIO * HEAD), lambda h: (0, h + first))
    whole = jax.ShapeDtypeStruct((ROWS, Q_HEADS * HEAD), BF16)
    row = pl.BlockSpec((1, ROWS), lambda h: (0, 0))
    return pl.pallas_call(
        finish_rows_kernel,
        grid=(count,),
        in_specs=[row, row, block]
        + [pl.BlockSpec((GROUPS, CHUNK, 2 * WIDE), lambda h: (0, 0, h))]
        + [pl.BlockSpec(memory_space=pl.ANY)] * len(earlier),
        out_specs=[block, block],
        out_shape=[whole, whole],
        scratch_shapes=[pltpu.VMEM((TALL, TALL), BF16)],
        input_output_aliases={4 + n: n for n in range(len(earlier))},
        compiler_params=params(),
        cost_estimate=cost(count * 2 * TALL * TALL * 2 * WIDE, count * (5 << 18)),
        name="finish_rows",
    )(order, gain, query, received, *earlier)


def finish_kv_kernel(order_ref, gain_ref, k_ref, in_ref, dk_ref, dv_ref):
    half = KV_HEADS * HEAD // 2
    gain = gain_ref[...]
    rows = dot(home_matrix(order_ref), in_ref[...].reshape(TALL, half), MM)
    for h in range(KV_HEADS):
        part, cols = h // (KV_HEADS // 2), head_cols(h % (KV_HEADS // 2))
        dy = rows[part * ROWS : (part + 1) * ROWS, cols]
        dk_ref[:, head_cols(h)] = norm_back(
            k_ref[:, head_cols(h)].astype(F32), gain, dy
        ).astype(BF16)
    dv_ref[:, :half] = rows[2 * ROWS : 3 * ROWS].astype(BF16)
    dv_ref[:, half:] = rows[3 * ROWS :].astype(BF16)


def finish_kv(order, gain, key_projection, received):
    whole = jax.ShapeDtypeStruct((ROWS, KV_HEADS * HEAD), BF16)
    return pl.pallas_call(
        finish_kv_kernel,
        out_shape=[whole, whole],
        compiler_params=params(),
        cost_estimate=cost(2 * TALL**3, 3 << 19),
        name="finish_kv",
    )(order, gain, key_projection, received)


def exchange(array):
    return lax.all_to_all(array, "dp", split_axis=0, concat_axis=0, tiled=True)


def along(array, step):
    count = lax.axis_size("seq")
    return lax.ppermute(array, "seq", [(i, (i + step) % count) for i in range(count)])


def after(array, other):
    return array if other is None else lax.optimization_barrier((array, other))[0]


def per_device(
    query, key_projection, value, d_out, q_gain, key_norm_gain, seq_lengths, send_order, recv_order
):
    leaving = send_order.reshape(1, ROWS)
    arriving = recv_order.reshape(1, ROWS)
    q_gain = q_gain.reshape(1, HEAD)
    k_gain = key_norm_gain.reshape(1, HEAD)
    place = lax.axis_index("seq").astype(jnp.int32)
    meta = jnp.concatenate([seq_lengths[0], place[None]])

    sent_small = send(
        leaving, q_gain, query, d_out, 0, SMALL, kv=(k_gain, key_projection, value)
    )
    sent_large = send(leaving, q_gain, query, d_out, SMALL, LARGE)
    small_rows = exchange(sent_small)
    large_rows = exchange(after(sent_large, small_rows))

    small, large = ([block] for block in sort_kv(arriving, small_rows))
    for _ in range(BACK):
        small.append(along(small[-1], 1))
        large.append(along(large[-1], 1))

    def back_along(parts):
        totals = parts[:1]
        for part in parts[1:-1]:
            totals.append((along(totals[-1], -1).astype(F32) + part).astype(BF16))
        return totals + [along(totals[-1], -1)], parts[-1]

    small_result, *parts = attend(meta, arriving, small_rows, small[::-1], SMALL, WEIGHTS[0])
    small_sums, small_own = back_along(parts)
    small_result = after(after(small_result, large_rows), large[BACK - 1])
    small_back = exchange(small_result)
    large[-1] = after(large[-1], small_sums[1])
    large_result, *parts = attend(meta, arriving, large_rows, large[::-1], LARGE, WEIGHTS[1])
    large_sums, large_own = back_along(parts)
    large_back = exchange(after(large_result, small_back))
    kv_back = return_kv(arriving, (small_sums[-1], large_sums[-1]), (small_own, large_own))
    kv_back = exchange(after(kv_back, large_back))

    outs = finish_rows(leaving, q_gain, query, small_back, 0, SMALL)
    outs = finish_rows(leaving, q_gain, query, large_back, SMALL, LARGE, earlier=outs)
    return *outs, *finish_kv(leaving, k_gain, key_projection, kv_back)


def solution(mesh):
    rows = P(("dp", "seq"), None)
    in_specs = (rows, rows, rows, rows, P(), P(), P("dp", None)) + (P("dp", "seq", None),) * 2
    return jax.shard_map(
        per_device, mesh=mesh, in_specs=in_specs, out_specs=(rows,) * 4, check_vma=False
    )
```

```python
import functools

import jax
import jax.numpy as jnp
from jax import lax
from jax.experimental import pallas as pl
from jax.experimental.pallas import tpu as pltpu
from jax.sharding import PartitionSpec as P

Q_HEADS = 64
KV_HEADS = 8
HEAD = 128
RATIO = Q_HEADS // KV_HEADS
EPS = 1e-06
ROWS = 128
GROUPS = 32
SHARE = ROWS // GROUPS
SPLIT = 4
CHUNK = SHARE * SPLIT
TALL = GROUPS * CHUNK
WIDE = 2 * HEAD
BACK = 4
WINDOW = (BACK + 1) * ROWS
SCALE = HEAD ** (-0.5)
LOG2E = 1.4426950408889634
FIRST = 6
LAST = KV_HEADS - FIRST
WEIGHTS = (12, 36)
VMEM_LIMIT = 52 * 1024 * 1024
VMEM_WHOLE = 62 * 1024 * 1024
F32 = jnp.float32
BF16 = jnp.bfloat16


def params(limit=VMEM_LIMIT):
    return pltpu.CompilerParams(vmem_limit_bytes=limit)


def cost(flops, moved, trans=0):
    return pl.CostEstimate(flops=int(flops), bytes_accessed=int(moved), transcendentals=int(trans))


def dot(a, b, dims):
    return lax.dot_general(a, b, (dims, ((), ())), preferred_element_type=F32)


MM = ((1,), (0,))
MT = ((1,), (1,))
TM = ((0,), (0,))


def iota(shape, dim):
    return lax.broadcasted_iota(jnp.int32, shape, dim)


def tall_row(index):
    row = (index // CHUNK) * SHARE + index % SHARE
    part = (index // SHARE) % SPLIT
    return row, part


def home_matrix(order_ref):
    spread_row, _ = tall_row(iota((ROWS, TALL), 1))
    spread = (spread_row == iota((ROWS, TALL), 0)).astype(BF16)
    order = jnp.broadcast_to(order_ref[...].astype(F32), (16, ROWS)).astype(BF16)
    source = dot(order, spread, MM)[:1]
    _, part = tall_row(iota((1, TALL), 1))
    code = source + (part * ROWS).astype(F32)
    return (iota((TALL, TALL), 0).astype(F32) == code).astype(BF16)


def pack_matrix(order_ref):
    row, part = tall_row(iota((TALL, SPLIT * ROWS), 0))
    order = order_ref[...]
    code = jnp.concatenate([order + p * ROWS for p in range(SPLIT)], axis=1)
    return (row + part * ROWS == code).astype(BF16)


def norm(x, gain):
    factor = lax.rsqrt(jnp.mean(x * x, axis=-1, keepdims=True) + EPS)
    return x * factor * gain


def norm_back(x, gain, dy):
    factor = lax.rsqrt(jnp.mean(x * x, axis=-1, keepdims=True) + EPS)
    g = dy * gain
    inner = jnp.mean(x * g, axis=-1, keepdims=True)
    return factor * g - x * (factor * factor * factor * inner)


def head_cols(h):
    return slice(h * HEAD, (h + 1) * HEAD)


def send_kv_kernel(order_ref, gain_ref, k_ref, v_ref, out_ref):
    gain = gain_ref[...]
    kn = [
        norm(k_ref[:, head_cols(h)].astype(F32), gain).astype(BF16) for h in range(KV_HEADS)
    ]
    half = KV_HEADS * HEAD // 2
    stack = jnp.concatenate(
        [
            jnp.concatenate(kn[: KV_HEADS // 2], axis=1),
            jnp.concatenate(kn[KV_HEADS // 2 :], axis=1),
            v_ref[:, :half],
            v_ref[:, half:],
        ],
        axis=0,
    )
    sent = dot(home_matrix(order_ref), stack, TM).astype(BF16)
    out_ref[...] = sent.reshape(GROUPS, CHUNK, half)


def send_kv(order, gain, key_projection, value):
    half = KV_HEADS * HEAD // 2
    return pl.pallas_call(
        send_kv_kernel,
        out_shape=jax.ShapeDtypeStruct((GROUPS, CHUNK, half), BF16),
        compiler_params=params(VMEM_WHOLE),
        cost_estimate=cost(2 * TALL * TALL * half, 3 << 19),
        name="send_kv",
    )(order, gain, key_projection, value)


def send_rows_kernel(order_ref, gain_ref, q_ref, d_ref, out_ref, home_ref):
    @pl.when(pl.program_id(0) == 0)
    def _():
        home_ref[...] = home_matrix(order_ref)

    gain = gain_ref[...]
    qn = [norm(q_ref[:, head_cols(h)].astype(F32), gain).astype(BF16) for h in range(RATIO)]
    stack = jnp.concatenate(
        [
            jnp.concatenate(
                [qn[2 * p], qn[2 * p + 1], d_ref[:, p * WIDE : (p + 1) * WIDE]], axis=1
            )
            for p in range(SPLIT)
        ],
        axis=0,
    )
    sent = dot(home_ref[...], stack, TM).astype(BF16)
    out_ref[...] = sent.reshape(GROUPS, CHUNK, 2 * WIDE)


def send_rows(order, gain, query, d_out, first, count):
    return pl.pallas_call(
        send_rows_kernel,
        grid=(count,),
        in_specs=[
            pl.BlockSpec((1, ROWS), lambda h: (0, 0)),
            pl.BlockSpec((1, HEAD), lambda h: (0, 0)),
            pl.BlockSpec((ROWS, RATIO * HEAD), lambda h: (0, h + first)),
            pl.BlockSpec((ROWS, RATIO * HEAD), lambda h: (0, h + first)),
        ],
        out_specs=pl.BlockSpec((GROUPS, CHUNK, 2 * WIDE), lambda h: (0, 0, h)),
        out_shape=jax.ShapeDtypeStruct((GROUPS, CHUNK, count * 2 * WIDE), BF16),
        scratch_shapes=[pltpu.VMEM((TALL, TALL), BF16)],
        compiler_params=params(VMEM_WHOLE),
        cost_estimate=cost(count * 2 * TALL * TALL * 2 * WIDE, count << 20),
        name="send_rows",
    )(order, gain, query, d_out)


def sort_kv_kernel(order_ref, in_ref, k_ref, v_ref):
    half = KV_HEADS * HEAD // 2
    rows = dot(pack_matrix(order_ref), in_ref[...].reshape(TALL, half), TM).astype(BF16)
    for n, ref in enumerate((k_ref, v_ref)):
        ref[:, :half] = rows[2 * n * ROWS : (2 * n + 1) * ROWS]
        ref[:, half:] = rows[(2 * n + 1) * ROWS : (2 * n + 2) * ROWS]


def sort_kv(order, received):
    return pl.pallas_call(
        sort_kv_kernel,
        out_shape=[jax.ShapeDtypeStruct((ROWS, KV_HEADS * HEAD), BF16)] * 2,
        compiler_params=params(),
        cost_estimate=cost(2 * TALL**3, 1 << 20),
        name="sort_kv",
    )(order, received)


def attend_kernel(meta_ref, order_ref, qd_ref, *refs):
    k_refs, v_refs = refs[: BACK + 1], refs[BACK + 1 : 2 * BACK + 2]
    out_ref, *part_refs, bias_ref = refs[-(BACK + 3) :]

    @pl.when(pl.program_id(0) == 0)
    def _():
        places = jnp.broadcast_to(iota((1, ROWS), 1).astype(F32), (16, ROWS)).astype(BF16)
        arrived = (iota((ROWS, ROWS), 0) == order_ref[...]).astype(BF16)
        place = dot(places, arrived, MT).astype(BF16)
        row, _ = tall_row(iota((ROWS, TALL), 1))
        spread = (row == iota((ROWS, TALL), 0)).astype(BF16)
        base = meta_ref[3] * ROWS
        position = dot(place, spread, MM)[:1] + base.astype(F32)
        end0 = meta_ref[0].astype(F32)
        end1 = (meta_ref[0] + meta_ref[1]).astype(F32)
        start = jnp.where(position < end0, 0.0, jnp.where(position < end1, end0, end1))
        key = (iota((WINDOW, TALL), 0) + (base - BACK * ROWS)).astype(F32)
        bias_ref[...] = jnp.where((key >= start) & (key <= position), 0.0, -1e30)

    kw = jnp.concatenate([r[...] for r in k_refs], axis=0)
    vw = jnp.concatenate([r[...] for r in v_refs], axis=0)

    def both(low):
        return jnp.concatenate(
            [
                qd_ref[:, :, low + e * HEAD : low + (e + 1) * HEAD].reshape(TALL, HEAD)
                for e in range(2)
            ],
            axis=0,
        )

    q, d = both(0), both(WIDE)
    scores = dot(kw, q, MT)
    d_weights = dot(vw, d, MT)
    bias = bias_ref[...]
    expo = jnp.exp2(scores * (SCALE * LOG2E) + jnp.concatenate([bias, bias], axis=1))
    weights = expo * (1.0 / jnp.sum(expo, axis=0, keepdims=True))
    low_weights = weights.astype(BF16)
    out = dot(vw, low_weights, TM).astype(BF16)
    delta = jnp.sum(d.astype(F32).T * out.astype(F32), axis=0, keepdims=True)
    d_scores = (weights * (d_weights - delta)).astype(BF16)
    dq = (dot(kw, d_scores, TM) * SCALE).astype(BF16)
    dk = dot(d_scores, q, MM) * SCALE
    dv = dot(low_weights, d, MM)
    for low, value in ((0, out.T), (WIDE, dq.T)):
        for e in range(2):
            out_ref[:, :, low + e * HEAD : low + (e + 1) * HEAD] = value[
                e * TALL : (e + 1) * TALL
            ].reshape(GROUPS, CHUNK, HEAD)
    for n, ref in enumerate(part_refs):
        ref[:, :HEAD] = dk[n * ROWS : (n + 1) * ROWS].astype(ref.dtype)
        ref[:, HEAD:] = dv[n * ROWS : (n + 1) * ROWS].astype(ref.dtype)


def attend(meta, order, received, keys, values, first, count, room, weight):
    head_spec = pl.BlockSpec((ROWS, HEAD), lambda h: (0, h + first))
    part_spec = pl.BlockSpec((ROWS, WIDE), lambda h: (0, h))
    rows_spec = pl.BlockSpec((GROUPS, CHUNK, 2 * WIDE), lambda h: (0, 0, h))
    elements = count * RATIO * ROWS * WINDOW
    return pl.pallas_call(
        attend_kernel,
        grid=(count,),
        in_specs=[
            pl.BlockSpec(memory_space=pltpu.SMEM),
            pl.BlockSpec((1, ROWS), lambda h: (0, 0)),
            rows_spec,
        ]
        + [head_spec] * (2 * BACK + 2),
        out_specs=[rows_spec] + [part_spec] * (BACK + 1),
        out_shape=[jax.ShapeDtypeStruct((GROUPS, CHUNK, (count + room) * 2 * WIDE), BF16)]
        + [
            jax.ShapeDtypeStruct((ROWS, count * WIDE), BF16 if n == 0 else F32)
            for n in range(BACK + 1)
        ],
        scratch_shapes=[pltpu.VMEM((WINDOW, TALL), F32)],
        compiler_params=params(),
        cost_estimate=cost(weight * elements * HEAD, count * (3 << 20), elements),
        name="attend",
    )(meta, order, received, *keys, *values)


def return_kv_kernel(order_ref, *refs):
    half = KV_HEADS * HEAD // 2
    count, out_ref = (len(refs) - 2) // 2, refs[-1]
    total = jnp.concatenate(
        [
            (got[...].astype(F32) + own[...]).astype(BF16)
            for got, own in zip(refs[:count], refs[count : 2 * count])
        ],
        axis=1,
    )

    def columns(which, part):
        heads = range(part * KV_HEADS // 2, (part + 1) * KV_HEADS // 2)
        return jnp.concatenate([total[:, head_cols(2 * h + which)] for h in heads], axis=1)

    stack = jnp.concatenate(
        [columns(which, part) for which in range(2) for part in range(2)], axis=0
    )
    rows = dot(pack_matrix(order_ref), stack, MM).astype(BF16)
    out_ref[...] = rows.reshape(GROUPS, CHUNK, half)


def return_kv(order, got, own, result):
    half = KV_HEADS * HEAD // 2
    place = result.shape[2] // half - 1
    small = [pl.BlockSpec(a.shape, lambda i: (0, 0)) for a in (order, *got, *own)]
    return pl.pallas_call(
        return_kv_kernel,
        grid=(1,),
        in_specs=small + [pl.BlockSpec(memory_space=pl.ANY)],
        out_specs=pl.BlockSpec((GROUPS, CHUNK, half), lambda i: (0, 0, place)),
        out_shape=jax.ShapeDtypeStruct(result.shape, BF16),
        input_output_aliases={len(small): 0},
        compiler_params=params(),
        cost_estimate=cost(2 * TALL**3, 3 << 20),
        name="return_kv",
    )(order, *got, *own, result)


def finish_rows_step(rows, gain, q_ref, out_ref, dq_ref):
    for part in range(SPLIT):
        mine = rows[part * ROWS : (part + 1) * ROWS]
        out_ref[:, part * WIDE : (part + 1) * WIDE] = mine[:, :WIDE].astype(BF16)
        for e in range(2):
            at = head_cols(2 * part + e)
            dy = mine[:, WIDE + e * HEAD : WIDE + (e + 1) * HEAD]
            dq_ref[:, at] = norm_back(q_ref[:, at].astype(F32), gain, dy).astype(BF16)


def finish_kv_step(rows, gain, k_ref, dk_ref, dv_ref):
    half = KV_HEADS * HEAD // 2
    for h in range(KV_HEADS):
        part, cols = h // (KV_HEADS // 2), head_cols(h % (KV_HEADS // 2))
        dy = rows[part * ROWS : (part + 1) * ROWS, cols]
        dk_ref[:, head_cols(h)] = norm_back(
            k_ref[:, head_cols(h)].astype(F32), gain, dy
        ).astype(BF16)
    dv_ref[:, :half] = rows[2 * ROWS : 3 * ROWS].astype(BF16)
    dv_ref[:, half:] = rows[3 * ROWS :].astype(BF16)


def finish_kernel(with_kv, order_ref, gain_ref, q_ref, in_ref, *refs):
    home_ref = refs[-1]
    step = pl.program_id(0)

    @pl.when(step == 0)
    def _():
        home_ref[...] = home_matrix(order_ref)

    rows = dot(home_ref[...], in_ref[...].reshape(TALL, 2 * WIDE), MM)
    if with_kv:
        k_gain_ref, k_ref, _, _, out_ref, dq_ref, dk_ref, dv_ref = refs[:-1]
        last = pl.num_programs(0) - 1

        @pl.when(step < last)
        def _():
            finish_rows_step(rows, gain_ref[...], q_ref, out_ref, dq_ref)

        @pl.when(step == last)
        def _():
            finish_kv_step(rows, k_gain_ref[...], k_ref, dk_ref, dv_ref)
    else:
        out_ref, dq_ref = refs[:-1]
        finish_rows_step(rows, gain_ref[...], q_ref, out_ref, dq_ref)


def finish(order, gain, query, received, first, count, kv=(), earlier=()):
    block = pl.BlockSpec((ROWS, RATIO * HEAD), lambda h: (0, jnp.minimum(h, count - 1) + first))
    whole = jax.ShapeDtypeStruct((ROWS, Q_HEADS * HEAD), BF16)
    row = pl.BlockSpec((1, ROWS), lambda h: (0, 0))
    kv_block = pl.BlockSpec((ROWS, KV_HEADS * HEAD), lambda h: (0, 0))
    kv_whole = jax.ShapeDtypeStruct((ROWS, KV_HEADS * HEAD), BF16)
    in_specs = [row, row, block, pl.BlockSpec((GROUPS, CHUNK, 2 * WIDE), lambda h: (0, 0, h))]
    if kv:
        in_specs += [row, kv_block] + [pl.BlockSpec(memory_space=pl.ANY)] * 2
    return pl.pallas_call(
        functools.partial(finish_kernel, bool(kv)),
        grid=(count + 1 if kv else count,),
        in_specs=in_specs,
        out_specs=[block, block] + ([kv_block] * 2 if kv else []),
        out_shape=[whole, whole] + ([kv_whole] * 2 if kv else []),
        scratch_shapes=[pltpu.VMEM((TALL, TALL), BF16)],
        input_output_aliases={6: 0, 7: 1} if kv else {},
        compiler_params=params(),
        cost_estimate=cost(count * 2 * TALL * TALL * 2 * WIDE, count * (5 << 18)),
        name="finish",
    )(order, gain, query, received, *kv, *earlier)


def exchange(array):
    return lax.all_to_all(array, "dp", split_axis=0, concat_axis=0, tiled=True)


def along(array, step):
    count = lax.axis_size("seq")
    return lax.ppermute(array, "seq", [(i, (i + step) % count) for i in range(count)])


def after(array, other):
    return array if other is None else lax.optimization_barrier((array, other))[0]


def per_device(
    query, key_projection, value, d_out, q_gain, key_norm_gain, seq_lengths, send_order, recv_order
):
    leaving = send_order.reshape(1, ROWS)
    arriving = recv_order.reshape(1, ROWS)
    q_gain = q_gain.reshape(1, HEAD)
    k_gain = key_norm_gain.reshape(1, HEAD)
    place = lax.axis_index("seq").astype(jnp.int32)
    meta = jnp.concatenate([seq_lengths[0], place[None]])
    counts = (FIRST, KV_HEADS - FIRST)
    starts = (0, FIRST)

    kv_sent = send_kv(leaving, k_gain, key_projection, value)
    kv_received = exchange(kv_sent)
    sent = [
        send_rows(leaving, q_gain, query, d_out, first, count)
        for first, count in zip(starts, counts)
    ]
    kv_received, *sent = lax.optimization_barrier((kv_received, *sent))
    received_first = exchange(sent[0])

    keys, values = ([block] for block in sort_kv(arriving, kv_received))
    for n in range(BACK):
        keys.append(along(after(keys[-1], values[n - 1] if n > 1 else None), 1))
        values.append(along(values[-1], 1))
    received_last = exchange(after(after(sent[1], received_first), values[BACK - 1]))

    def back_along(parts):
        totals = parts[:1]
        for part in parts[1:-1]:
            totals.append((along(totals[-1], -1).astype(F32) + part).astype(BF16))
        return totals + [along(totals[-1], -1)], parts[-1]

    result, *parts = attend(
        meta, arriving, received_first, keys[::-1], values[::-1], 0, FIRST, 0, WEIGHTS[0]
    )
    sums0, own0 = back_along(parts)
    back_first = exchange(result)
    keys[0] = after(keys[0], sums0[1])
    result, *parts = attend(
        meta, arriving, received_last, keys[::-1], values[::-1], FIRST, LAST, 1, WEIGHTS[1]
    )
    sums1, own1 = back_along(parts)
    merged = return_kv(arriving, (sums0[-1], sums1[-1]), (own0, own1), result)
    back_last = exchange(after(merged, back_first))

    outs = finish(leaving, q_gain, query, back_first, starts[0], counts[0])
    return tuple(
        finish(
            leaving,
            q_gain,
            query,
            back_last,
            starts[1],
            counts[1],
            kv=(k_gain, key_projection),
            earlier=outs,
        )
    )


def solution(mesh):
    rows = P(("dp", "seq"), None)
    in_specs = (rows, rows, rows, rows, P(), P(), P("dp", None)) + (P("dp", "seq", None),) * 2
    return jax.shard_map(
        per_device, mesh=mesh, in_specs=in_specs, out_specs=(rows,) * 4, check_vma=False
    )
```

```python
import functools

import jax
import jax.numpy as jnp
from jax import lax
from jax.experimental import pallas as pl
from jax.experimental.pallas import tpu as pltpu
from jax.sharding import PartitionSpec as P

Q_HEADS = 64
KV_HEADS = 8
HEAD = 128
RATIO = Q_HEADS // KV_HEADS
EPS = 1e-06
ROWS = 128
GROUPS = 32
SHARE = ROWS // GROUPS
SPLIT = 4
CHUNK = SHARE * SPLIT
TALL = GROUPS * CHUNK
WIDE = 2 * HEAD
BACK = 4
WINDOW = (BACK + 1) * ROWS
SCALE = HEAD ** (-0.5)
LOG2E = 1.4426950408889634
WEIGHT = 36
VMEM_LIMIT = 52 * 1024 * 1024
VMEM_WHOLE = 62 * 1024 * 1024
F32 = jnp.float32
BF16 = jnp.bfloat16


def params(limit=VMEM_LIMIT):
    return pltpu.CompilerParams(vmem_limit_bytes=limit)


def cost(flops, moved, trans=0):
    return pl.CostEstimate(flops=int(flops), bytes_accessed=int(moved), transcendentals=int(trans))


def dot(a, b, dims):
    return lax.dot_general(a, b, (dims, ((), ())), preferred_element_type=F32)


MM = ((1,), (0,))
MT = ((1,), (1,))
TM = ((0,), (0,))


def iota(shape, dim):
    return lax.broadcasted_iota(jnp.int32, shape, dim)


def tall_row(index):
    row = (index // CHUNK) * SHARE + index % SHARE
    part = (index // SHARE) % SPLIT
    return row, part


def home_matrix(order_ref):
    spread_row, _ = tall_row(iota((ROWS, TALL), 1))
    spread = (spread_row == iota((ROWS, TALL), 0)).astype(BF16)
    order = jnp.broadcast_to(order_ref[...].astype(F32), (16, ROWS)).astype(BF16)
    source = dot(order, spread, MM)[:1]
    _, part = tall_row(iota((1, TALL), 1))
    code = source + (part * ROWS).astype(F32)
    return (iota((TALL, TALL), 0).astype(F32) == code).astype(BF16)


def pack_matrix(order_ref):
    row, part = tall_row(iota((TALL, SPLIT * ROWS), 0))
    order = order_ref[...]
    code = jnp.concatenate([order + p * ROWS for p in range(SPLIT)], axis=1)
    return (row + part * ROWS == code).astype(BF16)


def norm(x, gain):
    factor = lax.rsqrt(jnp.mean(x * x, axis=-1, keepdims=True) + EPS)
    return x * factor * gain


def norm_back(x, gain, dy):
    factor = lax.rsqrt(jnp.mean(x * x, axis=-1, keepdims=True) + EPS)
    g = dy * gain
    inner = jnp.mean(x * g, axis=-1, keepdims=True)
    return factor * g - x * (factor * factor * factor * inner)


def head_cols(h):
    return slice(h * HEAD, (h + 1) * HEAD)


def send_kv_kernel(order_ref, gain_ref, k_ref, v_ref, out_ref):
    gain = gain_ref[...]
    kn = [
        norm(k_ref[:, head_cols(h)].astype(F32), gain).astype(BF16) for h in range(KV_HEADS)
    ]
    half = KV_HEADS * HEAD // 2
    stack = jnp.concatenate(
        [
            jnp.concatenate(kn[: KV_HEADS // 2], axis=1),
            jnp.concatenate(kn[KV_HEADS // 2 :], axis=1),
            v_ref[:, :half],
            v_ref[:, half:],
        ],
        axis=0,
    )
    sent = dot(home_matrix(order_ref), stack, TM).astype(BF16)
    out_ref[...] = sent.reshape(GROUPS, CHUNK, half)


def send_kv(order, gain, key_projection, value):
    half = KV_HEADS * HEAD // 2
    return pl.pallas_call(
        send_kv_kernel,
        out_shape=jax.ShapeDtypeStruct((GROUPS, CHUNK, half), BF16),
        compiler_params=params(VMEM_WHOLE),
        cost_estimate=cost(2 * TALL * TALL * half, 3 << 19),
        name="send_kv",
    )(order, gain, key_projection, value)


def send_rows_kernel(order_ref, gain_ref, q_ref, d_ref, out_ref, home_ref):
    @pl.when(pl.program_id(0) == 0)
    def _():
        home_ref[...] = home_matrix(order_ref)

    gain = gain_ref[...]
    qn = [norm(q_ref[:, head_cols(h)].astype(F32), gain).astype(BF16) for h in range(RATIO)]
    stack = jnp.concatenate(
        [
            jnp.concatenate(
                [qn[2 * p], qn[2 * p + 1], d_ref[:, p * WIDE : (p + 1) * WIDE]], axis=1
            )
            for p in range(SPLIT)
        ],
        axis=0,
    )
    sent = dot(home_ref[...], stack, TM).astype(BF16)
    out_ref[...] = sent.reshape(GROUPS, CHUNK, 2 * WIDE)


def send_rows(order, gain, query, d_out):
    row = pl.BlockSpec((1, ROWS), lambda h: (0, 0))
    block = pl.BlockSpec((ROWS, RATIO * HEAD), lambda h: (0, h))
    return pl.pallas_call(
        send_rows_kernel,
        grid=(KV_HEADS,),
        in_specs=[row, row, block, block],
        out_specs=pl.BlockSpec((GROUPS, CHUNK, 2 * WIDE), lambda h: (0, 0, h)),
        out_shape=jax.ShapeDtypeStruct((GROUPS, CHUNK, KV_HEADS * 2 * WIDE), BF16),
        scratch_shapes=[pltpu.VMEM((TALL, TALL), BF16)],
        compiler_params=params(VMEM_WHOLE),
        cost_estimate=cost(KV_HEADS * 2 * TALL * TALL * 2 * WIDE, KV_HEADS << 20),
        name="send_rows",
    )(order, gain, query, d_out)


def sort_kv_kernel(order_ref, in_ref, k_ref, v_ref):
    half = KV_HEADS * HEAD // 2
    rows = dot(pack_matrix(order_ref), in_ref[...].reshape(TALL, half), TM).astype(BF16)
    for n, ref in enumerate((k_ref, v_ref)):
        ref[:, :half] = rows[2 * n * ROWS : (2 * n + 1) * ROWS]
        ref[:, half:] = rows[(2 * n + 1) * ROWS : (2 * n + 2) * ROWS]


def sort_kv(order, received):
    return pl.pallas_call(
        sort_kv_kernel,
        out_shape=[jax.ShapeDtypeStruct((ROWS, KV_HEADS * HEAD), BF16)] * 2,
        compiler_params=params(),
        cost_estimate=cost(2 * TALL**3, 1 << 20),
        name="sort_kv",
    )(order, received)


def attend_kernel(meta_ref, order_ref, qd_ref, *refs):
    k_refs, v_refs = refs[: BACK + 1], refs[BACK + 1 : 2 * BACK + 2]
    out_ref, *part_refs, bias_ref = refs[2 * BACK + 2 :]
    dk_refs, dv_refs = part_refs[: BACK + 1], part_refs[BACK + 1 :]

    @pl.when(pl.program_id(0) == 0)
    def _():
        places = jnp.broadcast_to(iota((1, ROWS), 1).astype(F32), (16, ROWS)).astype(BF16)
        arrived = (iota((ROWS, ROWS), 0) == order_ref[...]).astype(BF16)
        place = dot(places, arrived, MT).astype(BF16)
        row, _ = tall_row(iota((ROWS, TALL), 1))
        spread = (row == iota((ROWS, TALL), 0)).astype(BF16)
        base = meta_ref[3] * ROWS
        position = dot(place, spread, MM)[:1] + base.astype(F32)
        end0 = meta_ref[0].astype(F32)
        end1 = (meta_ref[0] + meta_ref[1]).astype(F32)
        start = jnp.where(position < end0, 0.0, jnp.where(position < end1, end0, end1))
        key = (iota((WINDOW, TALL), 0) + (base - BACK * ROWS)).astype(F32)
        bias_ref[...] = jnp.where((key >= start) & (key <= position), 0.0, -1e30)

    kw = jnp.concatenate([r[...] for r in k_refs], axis=0)
    vw = jnp.concatenate([r[...] for r in v_refs], axis=0)

    def both(low):
        return jnp.concatenate(
            [
                qd_ref[:, :, low + e * HEAD : low + (e + 1) * HEAD].reshape(TALL, HEAD)
                for e in range(2)
            ],
            axis=0,
        )

    q, d = both(0), both(WIDE)
    scores = dot(kw, q, MT)
    d_weights = dot(vw, d, MT)
    bias = bias_ref[...]
    expo = jnp.exp2(scores * (SCALE * LOG2E) + jnp.concatenate([bias, bias], axis=1))
    weights = expo * (1.0 / jnp.sum(expo, axis=0, keepdims=True))
    low_weights = weights.astype(BF16)
    out = dot(vw, low_weights, TM).astype(BF16)
    delta = jnp.sum(d.astype(F32).T * out.astype(F32), axis=0, keepdims=True)
    d_scores = (weights * (d_weights - delta)).astype(BF16)
    dq = (dot(kw, d_scores, TM) * SCALE).astype(BF16)
    dk = dot(d_scores, q, MM) * SCALE
    dv = dot(low_weights, d, MM)
    for low, value in ((0, out.T), (WIDE, dq.T)):
        for e in range(2):
            out_ref[:, :, low + e * HEAD : low + (e + 1) * HEAD] = value[
                e * TALL : (e + 1) * TALL
            ].reshape(GROUPS, CHUNK, HEAD)
    for whole, parts in ((dk, dk_refs), (dv, dv_refs)):
        for n, ref in enumerate(parts):
            ref[...] = whole[n * ROWS : (n + 1) * ROWS].astype(ref.dtype)


def attend(meta, order, received, keys, values):
    head_spec = pl.BlockSpec((ROWS, HEAD), lambda h: (0, h))
    rows_spec = pl.BlockSpec((GROUPS, CHUNK, 2 * WIDE), lambda h: (0, 0, h))
    elements = Q_HEADS * ROWS * WINDOW
    parts = [
        jax.ShapeDtypeStruct((ROWS, KV_HEADS * HEAD), BF16 if n == 0 else F32)
        for n in range(BACK + 1)
    ]
    out, *parts = pl.pallas_call(
        attend_kernel,
        grid=(KV_HEADS,),
        in_specs=[
            pl.BlockSpec(memory_space=pltpu.SMEM),
            pl.BlockSpec((1, ROWS), lambda h: (0, 0)),
            rows_spec,
        ]
        + [head_spec] * (2 * BACK + 2),
        out_specs=[rows_spec] + [head_spec] * (2 * BACK + 2),
        out_shape=[jax.ShapeDtypeStruct(received.shape, BF16)] + parts * 2,
        scratch_shapes=[pltpu.VMEM((WINDOW, TALL), F32)],
        compiler_params=params(),
        cost_estimate=cost(WEIGHT * elements * HEAD, 3 << 23, elements),
        name="attend",
    )(meta, order, received, *keys, *values)
    return out, parts[: BACK + 1], parts[BACK + 1 :]


def return_kv_kernel(order_ref, dk_ref, dv_ref, own_dk_ref, own_dv_ref, out_ref):
    half = KV_HEADS * HEAD // 2
    stack = []
    for got, own in ((dk_ref, own_dk_ref), (dv_ref, own_dv_ref)):
        total = (got[...].astype(F32) + own[...]).astype(BF16)
        stack += [total[:, :half], total[:, half:]]
    rows = dot(pack_matrix(order_ref), jnp.concatenate(stack, axis=0), MM).astype(BF16)
    out_ref[...] = rows.reshape(GROUPS, CHUNK, half)


def return_kv(order, *sums):
    half = KV_HEADS * HEAD // 2
    return pl.pallas_call(
        return_kv_kernel,
        out_shape=jax.ShapeDtypeStruct((GROUPS, CHUNK, half), BF16),
        compiler_params=params(),
        cost_estimate=cost(2 * TALL**3, 3 << 20),
        name="return_kv",
    )(order, *sums)


def finish_rows_step(rows, gain, q_ref, out_ref, dq_ref):
    for part in range(SPLIT):
        mine = rows[part * ROWS : (part + 1) * ROWS]
        out_ref[:, part * WIDE : (part + 1) * WIDE] = mine[:, :WIDE].astype(BF16)
        for e in range(2):
            at = head_cols(2 * part + e)
            dy = mine[:, WIDE + e * HEAD : WIDE + (e + 1) * HEAD]
            dq_ref[:, at] = norm_back(q_ref[:, at].astype(F32), gain, dy).astype(BF16)


def finish_rows_kernel(order_ref, gain_ref, q_ref, in_ref, *refs):
    out_ref, dq_ref, home_ref = refs

    @pl.when(pl.program_id(0) == 0)
    def _():
        home_ref[...] = home_matrix(order_ref)

    rows = dot(home_ref[...], in_ref[...].reshape(TALL, 2 * WIDE), MM)
    finish_rows_step(rows, gain_ref[...], q_ref, out_ref, dq_ref)


def finish_rows(order, gain, query, received):
    block = pl.BlockSpec((ROWS, RATIO * HEAD), lambda h: (0, h))
    whole = jax.ShapeDtypeStruct((ROWS, Q_HEADS * HEAD), BF16)
    row = pl.BlockSpec((1, ROWS), lambda h: (0, 0))
    return pl.pallas_call(
        finish_rows_kernel,
        grid=(KV_HEADS,),
        in_specs=[row, row, block]
        + [pl.BlockSpec((GROUPS, CHUNK, 2 * WIDE), lambda h: (0, 0, h))],
        out_specs=[block, block],
        out_shape=[whole, whole],
        scratch_shapes=[pltpu.VMEM((TALL, TALL), BF16)],
        compiler_params=params(),
        cost_estimate=cost(KV_HEADS * 2 * TALL * TALL * 2 * WIDE, KV_HEADS * (5 << 18)),
        name="finish_rows",
    )(order, gain, query, received)


def finish_kv_kernel(order_ref, gain_ref, k_ref, in_ref, dk_ref, dv_ref):
    half = KV_HEADS * HEAD // 2
    gain = gain_ref[...]
    rows = dot(home_matrix(order_ref), in_ref[...].reshape(TALL, half), MM)
    for h in range(KV_HEADS):
        part, cols = h // (KV_HEADS // 2), head_cols(h % (KV_HEADS // 2))
        dy = rows[part * ROWS : (part + 1) * ROWS, cols]
        dk_ref[:, head_cols(h)] = norm_back(
            k_ref[:, head_cols(h)].astype(F32), gain, dy
        ).astype(BF16)
    dv_ref[:, :half] = rows[2 * ROWS : 3 * ROWS].astype(BF16)
    dv_ref[:, half:] = rows[3 * ROWS :].astype(BF16)


def finish_kv(order, gain, key_projection, received):
    whole = jax.ShapeDtypeStruct((ROWS, KV_HEADS * HEAD), BF16)
    return pl.pallas_call(
        finish_kv_kernel,
        out_shape=[whole, whole],
        compiler_params=params(),
        cost_estimate=cost(2 * TALL**3, 3 << 19),
        name="finish_kv",
    )(order, gain, key_projection, received)


def exchange(array):
    return lax.all_to_all(array, "dp", split_axis=0, concat_axis=0, tiled=True)


def along(array, step):
    count = lax.axis_size("seq")
    return lax.ppermute(array, "seq", [(i, (i + step) % count) for i in range(count)])


def after(array, other):
    return array if other is None else lax.optimization_barrier((array, other))[0]


def per_device(
    query, key_projection, value, d_out, q_gain, key_norm_gain, seq_lengths, send_order, recv_order
):
    leaving = send_order.reshape(1, ROWS)
    arriving = recv_order.reshape(1, ROWS)
    q_gain = q_gain.reshape(1, HEAD)
    k_gain = key_norm_gain.reshape(1, HEAD)
    place = lax.axis_index("seq").astype(jnp.int32)
    meta = jnp.concatenate([seq_lengths[0], place[None]])

    kv_received = exchange(send_kv(leaving, k_gain, key_projection, value))
    sent = send_rows(leaving, q_gain, query, d_out)
    keys, values = ([block] for block in sort_kv(arriving, kv_received))
    received = exchange(after(sent, keys[0]))

    for n in range(BACK):
        keys.append(along(after(keys[-1], values[n - 1] if n > 1 else None), 1))
        values.append(along(values[-1], 1))

    result, dk_parts, dv_parts = attend(meta, arriving, received, keys[::-1], values[::-1])
    back = exchange(result)

    dk, dv = dk_parts[0], dv_parts[0]
    for n in range(1, BACK):
        dk = (along(dk, -1).astype(F32) + dk_parts[n]).astype(BF16)
        dv = (along(dv, -1).astype(F32) + dv_parts[n]).astype(BF16)
    sums = along(dk, -1), along(dv, -1), dk_parts[-1], dv_parts[-1]
    kv_back = exchange(after(return_kv(arriving, *sums), back))

    outs = finish_rows(leaving, q_gain, query, back)
    return *outs, *finish_kv(leaving, k_gain, key_projection, kv_back)


def solution(mesh):
    rows = P(("dp", "seq"), None)
    in_specs = (rows, rows, rows, rows, P(), P(), P("dp", None)) + (P("dp", "seq", None),) * 2
    return jax.shard_map(
        per_device, mesh=mesh, in_specs=in_specs, out_specs=(rows,) * 4, check_vma=False
    )
```

```python
import functools

import jax
import jax.numpy as jnp
from jax import lax
from jax.experimental import pallas as pl
from jax.experimental.pallas import tpu as pltpu
from jax.sharding import PartitionSpec as P

Q_HEADS = 64
KV_HEADS = 8
HEAD = 128
RATIO = Q_HEADS // KV_HEADS
EPS = 1e-06
ROWS = 128
GROUPS = 32
SHARE = ROWS // GROUPS
SPLIT = 4
CHUNK = SHARE * SPLIT
TALL = GROUPS * CHUNK
WIDE = 2 * HEAD
BACK = 4
WINDOW = (BACK + 1) * ROWS
SCALE = HEAD ** (-0.5)
LOG2E = 1.4426950408889634
FIRST = 6
LAST = KV_HEADS - FIRST
WEIGHTS = (12, 36)
VMEM_LIMIT = 52 * 1024 * 1024
VMEM_WHOLE = 62 * 1024 * 1024
F32 = jnp.float32
BF16 = jnp.bfloat16


def params(limit=VMEM_LIMIT):
    return pltpu.CompilerParams(vmem_limit_bytes=limit)


def cost(flops, moved, trans=0):
    return pl.CostEstimate(flops=int(flops), bytes_accessed=int(moved), transcendentals=int(trans))


def dot(a, b, dims):
    return lax.dot_general(a, b, (dims, ((), ())), preferred_element_type=F32)


MM = ((1,), (0,))
MT = ((1,), (1,))
TM = ((0,), (0,))


def iota(shape, dim):
    return lax.broadcasted_iota(jnp.int32, shape, dim)


def tall_row(index):
    row = (index // CHUNK) * SHARE + index % SHARE
    part = (index // SHARE) % SPLIT
    return row, part


def home_matrix(order_ref):
    spread_row, _ = tall_row(iota((ROWS, TALL), 1))
    spread = (spread_row == iota((ROWS, TALL), 0)).astype(BF16)
    order = jnp.broadcast_to(order_ref[...].astype(F32), (16, ROWS)).astype(BF16)
    source = dot(order, spread, MM)[:1]
    _, part = tall_row(iota((1, TALL), 1))
    code = source + (part * ROWS).astype(F32)
    return (iota((TALL, TALL), 0).astype(F32) == code).astype(BF16)


def pack_matrix(order_ref):
    row, part = tall_row(iota((TALL, SPLIT * ROWS), 0))
    order = order_ref[...]
    code = jnp.concatenate([order + p * ROWS for p in range(SPLIT)], axis=1)
    return (row + part * ROWS == code).astype(BF16)


def norm(x, gain):
    factor = lax.rsqrt(jnp.mean(x * x, axis=-1, keepdims=True) + EPS)
    return x * factor * gain


def norm_back(x, gain, dy):
    factor = lax.rsqrt(jnp.mean(x * x, axis=-1, keepdims=True) + EPS)
    g = dy * gain
    inner = jnp.mean(x * g, axis=-1, keepdims=True)
    return factor * g - x * (factor * factor * factor * inner)


def head_cols(h):
    return slice(h * HEAD, (h + 1) * HEAD)


def send_kv_kernel(order_ref, gain_ref, k_ref, v_ref, out_ref):
    gain = gain_ref[...]
    kn = [
        norm(k_ref[:, head_cols(h)].astype(F32), gain).astype(BF16) for h in range(KV_HEADS)
    ]
    half = KV_HEADS * HEAD // 2
    stack = jnp.concatenate(
        [
            jnp.concatenate(kn[: KV_HEADS // 2], axis=1),
            jnp.concatenate(kn[KV_HEADS // 2 :], axis=1),
            v_ref[:, :half],
            v_ref[:, half:],
        ],
        axis=0,
    )
    sent = dot(home_matrix(order_ref), stack, TM).astype(BF16)
    out_ref[...] = sent.reshape(GROUPS, CHUNK, half)


def send_kv(order, gain, key_projection, value):
    half = KV_HEADS * HEAD // 2
    return pl.pallas_call(
        send_kv_kernel,
        out_shape=jax.ShapeDtypeStruct((GROUPS, CHUNK, half), BF16),
        compiler_params=params(VMEM_WHOLE),
        cost_estimate=cost(2 * TALL * TALL * half, 3 << 19),
        name="send_kv",
    )(order, gain, key_projection, value)


def send_rows_kernel(order_ref, gain_ref, q_ref, d_ref, out_ref, home_ref):
    @pl.when(pl.program_id(0) == 0)
    def _():
        home_ref[...] = home_matrix(order_ref)

    gain = gain_ref[...]
    qn = [norm(q_ref[:, head_cols(h)].astype(F32), gain).astype(BF16) for h in range(RATIO)]
    stack = jnp.concatenate(
        [
            jnp.concatenate(
                [qn[2 * p], qn[2 * p + 1], d_ref[:, p * WIDE : (p + 1) * WIDE]], axis=1
            )
            for p in range(SPLIT)
        ],
        axis=0,
    )
    sent = dot(home_ref[...], stack, TM).astype(BF16)
    out_ref[...] = sent.reshape(GROUPS, CHUNK, 2 * WIDE)


def send_rows(order, gain, query, d_out, first, count):
    return pl.pallas_call(
        send_rows_kernel,
        grid=(count,),
        in_specs=[
            pl.BlockSpec((1, ROWS), lambda h: (0, 0)),
            pl.BlockSpec((1, HEAD), lambda h: (0, 0)),
            pl.BlockSpec((ROWS, RATIO * HEAD), lambda h: (0, h + first)),
            pl.BlockSpec((ROWS, RATIO * HEAD), lambda h: (0, h + first)),
        ],
        out_specs=pl.BlockSpec((GROUPS, CHUNK, 2 * WIDE), lambda h: (0, 0, h)),
        out_shape=jax.ShapeDtypeStruct((GROUPS, CHUNK, count * 2 * WIDE), BF16),
        scratch_shapes=[pltpu.VMEM((TALL, TALL), BF16)],
        compiler_params=params(VMEM_WHOLE),
        cost_estimate=cost(count * 2 * TALL * TALL * 2 * WIDE, count << 20),
        name="send_rows",
    )(order, gain, query, d_out)


def sort_kv_kernel(order_ref, in_ref, k_ref, v_ref):
    half = KV_HEADS * HEAD // 2
    rows = dot(pack_matrix(order_ref), in_ref[...].reshape(TALL, half), TM).astype(BF16)
    for n, ref in enumerate((k_ref, v_ref)):
        ref[:, :half] = rows[2 * n * ROWS : (2 * n + 1) * ROWS]
        ref[:, half:] = rows[(2 * n + 1) * ROWS : (2 * n + 2) * ROWS]


def sort_kv(order, received):
    return pl.pallas_call(
        sort_kv_kernel,
        out_shape=[jax.ShapeDtypeStruct((ROWS, KV_HEADS * HEAD), BF16)] * 2,
        compiler_params=params(),
        cost_estimate=cost(2 * TALL**3, 1 << 20),
        name="sort_kv",
    )(order, received)


def attend_kernel(meta_ref, order_ref, qd_ref, *refs):
    k_refs, v_refs = refs[: BACK + 1], refs[BACK + 1 : 2 * BACK + 2]
    out_ref, *part_refs, bias_ref = refs[-(BACK + 3) :]

    @pl.when(pl.program_id(0) == 0)
    def _():
        places = jnp.broadcast_to(iota((1, ROWS), 1).astype(F32), (16, ROWS)).astype(BF16)
        arrived = (iota((ROWS, ROWS), 0) == order_ref[...]).astype(BF16)
        place = dot(places, arrived, MT).astype(BF16)
        row, _ = tall_row(iota((ROWS, TALL), 1))
        spread = (row == iota((ROWS, TALL), 0)).astype(BF16)
        base = meta_ref[3] * ROWS
        position = dot(place, spread, MM)[:1] + base.astype(F32)
        end0 = meta_ref[0].astype(F32)
        end1 = (meta_ref[0] + meta_ref[1]).astype(F32)
        start = jnp.where(position < end0, 0.0, jnp.where(position < end1, end0, end1))
        key = (iota((WINDOW, TALL), 0) + (base - BACK * ROWS)).astype(F32)
        bias_ref[...] = jnp.where((key >= start) & (key <= position), 0.0, -1e30)

    kw = jnp.concatenate([r[...] for r in k_refs], axis=0)
    vw = jnp.concatenate([r[...] for r in v_refs], axis=0)

    def both(low):
        return jnp.concatenate(
            [
                qd_ref[:, :, low + e * HEAD : low + (e + 1) * HEAD].reshape(TALL, HEAD)
                for e in range(2)
            ],
            axis=0,
        )

    q, d = both(0), both(WIDE)
    scores = dot(kw, q, MT)
    d_weights = dot(vw, d, MT)
    bias = bias_ref[...]
    expo = jnp.exp2(scores * (SCALE * LOG2E) + jnp.concatenate([bias, bias], axis=1))
    weights = expo * (1.0 / jnp.sum(expo, axis=0, keepdims=True))
    low_weights = weights.astype(BF16)
    out = dot(vw, low_weights, TM).astype(BF16)
    delta = jnp.sum(d.astype(F32).T * out.astype(F32), axis=0, keepdims=True)
    d_scores = (weights * (d_weights - delta)).astype(BF16)
    dq = (dot(kw, d_scores, TM) * SCALE).astype(BF16)
    dk = dot(d_scores, q, MM) * SCALE
    dv = dot(low_weights, d, MM)
    for low, value in ((0, out.T), (WIDE, dq.T)):
        for e in range(2):
            out_ref[:, :, low + e * HEAD : low + (e + 1) * HEAD] = value[
                e * TALL : (e + 1) * TALL
            ].reshape(GROUPS, CHUNK, HEAD)
    for n, ref in enumerate(part_refs):
        ref[:, :HEAD] = dk[n * ROWS : (n + 1) * ROWS].astype(ref.dtype)
        ref[:, HEAD:] = dv[n * ROWS : (n + 1) * ROWS].astype(ref.dtype)


def attend(meta, order, received, keys, values, first, count, room, weight):
    head_spec = pl.BlockSpec((ROWS, HEAD), lambda h: (0, h + first))
    part_spec = pl.BlockSpec((ROWS, WIDE), lambda h: (0, h))
    rows_spec = pl.BlockSpec((GROUPS, CHUNK, 2 * WIDE), lambda h: (0, 0, h))
    elements = count * RATIO * ROWS * WINDOW
    return pl.pallas_call(
        attend_kernel,
        grid=(count,),
        in_specs=[
            pl.BlockSpec(memory_space=pltpu.SMEM),
            pl.BlockSpec((1, ROWS), lambda h: (0, 0)),
            rows_spec,
        ]
        + [head_spec] * (2 * BACK + 2),
        out_specs=[rows_spec] + [part_spec] * (BACK + 1),
        out_shape=[jax.ShapeDtypeStruct((GROUPS, CHUNK, (count + room) * 2 * WIDE), BF16)]
        + [
            jax.ShapeDtypeStruct((ROWS, count * WIDE), BF16 if n == 0 else F32)
            for n in range(BACK + 1)
        ],
        scratch_shapes=[pltpu.VMEM((WINDOW, TALL), F32)],
        compiler_params=params(),
        cost_estimate=cost(weight * elements * HEAD, count * (3 << 20), elements),
        name="attend",
    )(meta, order, received, *keys, *values)


def return_kv_kernel(order_ref, *refs):
    half = KV_HEADS * HEAD // 2
    count, out_ref = (len(refs) - 2) // 2, refs[-1]
    total = jnp.concatenate(
        [
            (got[...].astype(F32) + own[...]).astype(BF16)
            for got, own in zip(refs[:count], refs[count : 2 * count])
        ],
        axis=1,
    )

    def columns(which, part):
        heads = range(part * KV_HEADS // 2, (part + 1) * KV_HEADS // 2)
        return jnp.concatenate([total[:, head_cols(2 * h + which)] for h in heads], axis=1)

    stack = jnp.concatenate(
        [columns(which, part) for which in range(2) for part in range(2)], axis=0
    )
    rows = dot(pack_matrix(order_ref), stack, MM).astype(BF16)
    out_ref[...] = rows.reshape(GROUPS, CHUNK, half)


def return_kv(order, got, own, result):
    half = KV_HEADS * HEAD // 2
    place = result.shape[2] // half - 1
    small = [pl.BlockSpec(a.shape, lambda i: (0, 0)) for a in (order, *got, *own)]
    return pl.pallas_call(
        return_kv_kernel,
        grid=(1,),
        in_specs=small + [pl.BlockSpec(memory_space=pl.ANY)],
        out_specs=pl.BlockSpec((GROUPS, CHUNK, half), lambda i: (0, 0, place)),
        out_shape=jax.ShapeDtypeStruct(result.shape, BF16),
        input_output_aliases={len(small): 0},
        compiler_params=params(),
        cost_estimate=cost(2 * TALL**3, 3 << 20),
        name="return_kv",
    )(order, *got, *own, result)


def finish_rows_step(rows, gain, q_ref, out_ref, dq_ref):
    for part in range(SPLIT):
        mine = rows[part * ROWS : (part + 1) * ROWS]
        out_ref[:, part * WIDE : (part + 1) * WIDE] = mine[:, :WIDE].astype(BF16)
        for e in range(2):
            at = head_cols(2 * part + e)
            dy = mine[:, WIDE + e * HEAD : WIDE + (e + 1) * HEAD]
            dq_ref[:, at] = norm_back(q_ref[:, at].astype(F32), gain, dy).astype(BF16)


def finish_kv_step(rows, gain, k_ref, dk_ref, dv_ref):
    half = KV_HEADS * HEAD // 2
    for h in range(KV_HEADS):
        part, cols = h // (KV_HEADS // 2), head_cols(h % (KV_HEADS // 2))
        dy = rows[part * ROWS : (part + 1) * ROWS, cols]
        dk_ref[:, head_cols(h)] = norm_back(
            k_ref[:, head_cols(h)].astype(F32), gain, dy
        ).astype(BF16)
    dv_ref[:, :half] = rows[2 * ROWS : 3 * ROWS].astype(BF16)
    dv_ref[:, half:] = rows[3 * ROWS :].astype(BF16)


def finish_kernel(with_kv, order_ref, gain_ref, q_ref, in_ref, *refs):
    home_ref = refs[-1]
    step = pl.program_id(0)

    @pl.when(step == 0)
    def _():
        home_ref[...] = home_matrix(order_ref)

    rows = dot(home_ref[...], in_ref[...].reshape(TALL, 2 * WIDE), MM)
    if with_kv:
        k_gain_ref, k_ref, _, _, out_ref, dq_ref, dk_ref, dv_ref = refs[:-1]
        last = pl.num_programs(0) - 1

        @pl.when(step < last)
        def _():
            finish_rows_step(rows, gain_ref[...], q_ref, out_ref, dq_ref)

        @pl.when(step == last)
        def _():
            finish_kv_step(rows, k_gain_ref[...], k_ref, dk_ref, dv_ref)
    else:
        out_ref, dq_ref = refs[:-1]
        finish_rows_step(rows, gain_ref[...], q_ref, out_ref, dq_ref)


def finish(order, gain, query, received, first, count, kv=(), earlier=()):
    block = pl.BlockSpec((ROWS, RATIO * HEAD), lambda h: (0, jnp.minimum(h, count - 1) + first))
    whole = jax.ShapeDtypeStruct((ROWS, Q_HEADS * HEAD), BF16)
    row = pl.BlockSpec((1, ROWS), lambda h: (0, 0))
    kv_block = pl.BlockSpec((ROWS, KV_HEADS * HEAD), lambda h: (0, 0))
    kv_whole = jax.ShapeDtypeStruct((ROWS, KV_HEADS * HEAD), BF16)
    in_specs = [row, row, block, pl.BlockSpec((GROUPS, CHUNK, 2 * WIDE), lambda h: (0, 0, h))]
    if kv:
        in_specs += [row, kv_block] + [pl.BlockSpec(memory_space=pl.ANY)] * 2
    return pl.pallas_call(
        functools.partial(finish_kernel, bool(kv)),
        grid=(count + 1 if kv else count,),
        in_specs=in_specs,
        out_specs=[block, block] + ([kv_block] * 2 if kv else []),
        out_shape=[whole, whole] + ([kv_whole] * 2 if kv else []),
        scratch_shapes=[pltpu.VMEM((TALL, TALL), BF16)],
        input_output_aliases={6: 0, 7: 1} if kv else {},
        compiler_params=params(),
        cost_estimate=cost(count * 2 * TALL * TALL * 2 * WIDE, count * (5 << 18)),
        name="finish",
    )(order, gain, query, received, *kv, *earlier)


def exchange(array):
    return lax.all_to_all(array, "dp", split_axis=0, concat_axis=0, tiled=True)


def along(array, step):
    count = lax.axis_size("seq")
    return lax.ppermute(array, "seq", [(i, (i + step) % count) for i in range(count)])


def after(array, other):
    return array if other is None else lax.optimization_barrier((array, other))[0]


def per_device(
    query, key_projection, value, d_out, q_gain, key_norm_gain, seq_lengths, send_order, recv_order
):
    leaving = send_order.reshape(1, ROWS)
    arriving = recv_order.reshape(1, ROWS)
    q_gain = q_gain.reshape(1, HEAD)
    k_gain = key_norm_gain.reshape(1, HEAD)
    place = lax.axis_index("seq").astype(jnp.int32)
    meta = jnp.concatenate([seq_lengths[0], place[None]])
    kv_sent = send_kv(leaving, k_gain, key_projection, value)
    kv_received = exchange(kv_sent)
    sent_first = send_rows(leaving, q_gain, query, d_out, 0, FIRST)

    keys, values = ([block] for block in sort_kv(arriving, kv_received))
    received_first = exchange(after(sent_first, keys[0]))
    sent_last = send_rows(after(leaving, keys[0]), q_gain, query, d_out, FIRST, LAST)
    for n in range(BACK):
        keys.append(along(after(keys[-1], values[n - 1] if n > 1 else None), 1))
        values.append(along(values[-1], 1))
    received_last = exchange(after(after(sent_last, received_first), values[BACK - 1]))

    def back_along(parts):
        totals = parts[:1]
        for part in parts[1:-1]:
            totals.append((along(totals[-1], -1).astype(F32) + part).astype(BF16))
        return totals + [along(totals[-1], -1)], parts[-1]

    result, *parts = attend(
        meta, arriving, received_first, keys[::-1], values[::-1], 0, FIRST, 0, WEIGHTS[0]
    )
    sums0, own0 = back_along(parts)
    back_first = exchange(result)
    keys[0] = after(keys[0], sums0[1])
    result, *parts = attend(
        meta, arriving, received_last, keys[::-1], values[::-1], FIRST, LAST, 1, WEIGHTS[1]
    )
    sums1, own1 = back_along(parts)
    merged = return_kv(arriving, (sums0[-1], sums1[-1]), (own0, own1), result)
    back_last = exchange(after(merged, back_first))

    outs = finish(leaving, q_gain, query, back_first, 0, FIRST)
    return tuple(
        finish(
            leaving,
            q_gain,
            query,
            back_last,
            FIRST,
            LAST,
            kv=(k_gain, key_projection),
            earlier=outs,
        )
    )


def solution(mesh):
    rows = P(("dp", "seq"), None)
    in_specs = (rows, rows, rows, rows, P(), P(), P("dp", None)) + (P("dp", "seq", None),) * 2
    return jax.shard_map(
        per_device, mesh=mesh, in_specs=in_specs, out_specs=(rows,) * 4, check_vma=False
    )
```
